32 devices in a mesh: space: 16 (over z, y, core), mem: 2 (over x).
Axes of the slice: x: 2, y: 2, z: 4, core: 2. Of those that a mesh axis runs over, the one named last changes fastest.
Arguments:
- member_heat_solute: float32 [128, 2, 256, 128], P('mem', None, 'space'), may hold values from -6 to 6
- velocity: float32 [128, 256, 128], P('mem', 'space'), may hold values from 0.2 to 0.6
- phase_mask: int32 [256, 128], P('space'), may hold values 0 or 1
- obs_index: int32 [256], P('space'), may hold values from 0 to 2047
- obs_value: float32 [256], P('space'), may hold values from -6 to 6
- obs_error: float32 [256], P('space'), may hold values from 0.3 to 3
Outputs:
- analysis_hc: float32 [128, 2, 256, 128], P('mem', None, 'space')
- analysis_velocity: float32 [128, 256, 128], P('mem', 'space')
The draws below stay inside these ranges and needn't reach their ends.
Inputs may be any that keep to these rules, and one draw needn't show every extreme that they name: `obs_index`: observation o lies in slab o // 16; its entry counts cells row by row inside that slab.
All inputs are finite; a program needn't handle non-finite values. No bound on the sum of `phase_mask` on one device may be relied on, other than what follows from the above.
Results may differ from the reference program's by a relative error of at most 0.00015.
Values sent between devices are 32-bit elements; how exact they have to be, the bound alone decides.
A program may use at most 64 MiB of HBM per device.

```python
import math
import jax
import jax.numpy as jnp
from jax import lax

ENS = 128
LZ = 16
W = 128
NOBS = 16
NZ = 256
NOBS_ALL = 256


def set_ends(array, own_key, least, high):
    extent = array.shape
    index_at = [jax.random.randint(jax.random.fold_in(own_key, axis), (), 0, extent[axis]) for axis in range(len(extent))]
    array = array.at[tuple(index_at)].set(least)
    longest = extent.index(max(extent))
    index_at[longest] = (index_at[longest] + 1) % extent[longest]
    return array.at[tuple(index_at)].set(high)


def shard_levels(own_key, dims, pieces, smallest, largest):
    def one(dim, shards_of):
        draws = jax.random.uniform(jax.random.fold_in(jax.random.fold_in(own_key, 6), dim), (shards_of,), jnp.float32, smallest / len(pieces), largest / len(pieces))
        return jnp.repeat(jnp.exp(draws), dims[dim] // shards_of).reshape((-1,) + (1,) * (len(dims) - dim - 1))

    factor_of = one(*pieces[0])
    for cut in pieces[1:]:
        factor_of = factor_of * one(*cut)
    return factor_of


def scatter_about(stream_key, dims, width, most, shards=(), kind=jnp.bfloat16):
    loudness = shard_levels(stream_key, dims, shards, -0.22, 0.18) if shards else 1.0
    values = jax.random.normal(stream_key, dims, jnp.float32) * width * loudness
    return jnp.minimum(jnp.maximum(values, -most), most).astype(kind)


def setup_inputs(seed: int = 0) -> dict:
    seeds = jax.random.split(jax.random.key(seed), 7)
    return {
        "member_heat_solute": scatter_about(seeds[0], (ENS, 2, NZ, W), 1.0, 6.0, ((0, 2), (2, 16)), jnp.float32),
        "velocity": jnp.clip(0.2 + 0.400000021 * jax.random.uniform(seeds[1], (ENS, NZ, W), jnp.float32) ** shard_levels(seeds[1], (ENS, NZ, W), ((0, 2), (1, 16)), -0.2, 0.2), 0.2, 0.6),
        "phase_mask": set_ends((jax.random.randint(seeds[2], (NZ, W), 0, 3) < 1).astype(jnp.int32), jax.random.fold_in(seeds[2], 1), 0, 1),
        "obs_index": set_ends(jax.random.randint(seeds[3], (NOBS_ALL,), 0, LZ * W), jax.random.fold_in(seeds[3], 1), 0, (LZ * W) - 1).astype(jnp.int32),
        "obs_value": scatter_about(seeds[4], (NOBS_ALL,), 1.0, 6.0, ((0, 16),), jnp.float32),
        "obs_error": jnp.clip(jnp.exp(math.log(3.0) - 2.3025851 * jax.random.uniform(seeds[5], (NOBS_ALL,), jnp.float32) ** shard_levels(seeds[5], (NOBS_ALL,), ((0, 16),), -0.2, 0.2)), 0.3, 3.0),
    }


heat_diffusion = 0.15
advection = 0.4
solute_diffusion = 0.05
segregation = 0.3
momentum_diffusion = 0.1
darcy_drag = 0.5
mushy_ratio = 1.0 / 3.0

def lateral(field):
    left = jnp.concatenate([field[..., :1], field[..., :-1]], axis=-1)
    right = jnp.concatenate([field[..., 1:], field[..., -1:]], axis=-1)
    return left + right - 2.0 * field

def advance(padded_heat, padded_temp, padded_solute, padded_speed, factor, mushy):
    heat = padded_heat[..., 1:-1, :]
    temp = padded_temp[..., 1:-1, :]
    solute = padded_solute[..., 1:-1, :]
    speed = padded_speed[..., 1:-1, :]
    temp_lap = padded_temp[..., 2:, :] + padded_temp[..., :-2, :] - 2.0 * temp + lateral(temp)
    solute_lap = padded_solute[..., 2:, :] + padded_solute[..., :-2, :] - 2.0 * solute + lateral(solute)
    speed_lap = padded_speed[..., 2:, :] + padded_speed[..., :-2, :] - 2.0 * speed + lateral(speed)
    new_heat = heat + heat_diffusion * temp_lap - advection * speed * (heat - padded_heat[..., :-2, :])
    new_solute = solute + solute_diffusion * solute_lap - advection * speed * (solute - padded_solute[..., :-2, :]) + segregation * mushy * (temp - solute)
    new_speed = speed + momentum_diffusion * speed_lap - darcy_drag * mushy * speed
    return (new_heat, new_solute, new_speed)

def pad_rows(field):
    return jnp.pad(field, ((1, 1), (0, 0)))

def analysis_weights(gram, project):
    members = gram.shape[0]
    ident = jnp.eye(members, dtype=jnp.float32)
    lower = jnp.linalg.cholesky(ident + gram)
    mean_offset = jax.scipy.linalg.cho_solve((lower, True), project)
    inverse_root = jax.scipy.linalg.solve_triangular(lower.T, ident, lower=False)
    center = ident - 1.0 / members
    combined = mean_offset[:, None] / jnp.sqrt(jnp.float32(members - 1)) + inverse_root
    return 1.0 / members + jnp.dot(center, combined, precision=lax.Precision.HIGHEST)

def reference(member_heat_solute, velocity, phase_mask, obs_index, obs_value, obs_error):
    mushy = phase_mask.astype(jnp.float32)
    factor = 1.0 - mushy * (1.0 - mushy_ratio)
    slab_of = (jnp.arange(NOBS_ALL, dtype=jnp.int32) // NOBS).astype(jnp.int32)
    global_index = (slab_of * (LZ * W) + obs_index).astype(jnp.int32)

    def single_member(inputs):
        pair, speed = inputs
        heat = pair[0]
        solute = pair[1]
        for section in range(2):
            temp = heat * factor
            heat, solute, speed = advance(pad_rows(heat), pad_rows(temp), pad_rows(solute), pad_rows(speed), factor, mushy)
        temp = heat * factor
        seen = temp.reshape(-1)[global_index]
        return (jnp.stack([heat, solute]), speed, seen)
    predicted_heat_solute, predicted_speed, measured_values = lax.map(single_member, (member_heat_solute, velocity))
    members = measured_values.shape[0]
    mean_obs = lax.optimization_barrier(jnp.mean(measured_values, axis=0))
    spread = (measured_values - mean_obs[None, :]).T / (obs_error[:, None] * jnp.sqrt(jnp.float32(members - 1)))
    innovation = (obs_value - mean_obs) / obs_error
    gram = jnp.dot(spread.T, spread, precision=lax.Precision.HIGHEST)
    project = jnp.dot(spread.T, innovation, precision=lax.Precision.HIGHEST)
    mixing = analysis_weights(gram, project)
    field_stack = jnp.concatenate([predicted_heat_solute, predicted_speed[:, None]], axis=1)
    flat = field_stack.reshape(members, -1)
    mixed = jnp.dot(mixing.T, flat, precision=lax.Precision.HIGHEST).reshape(field_stack.shape)
    return (mixed[:, :2], mixed[:, 2])
```

```python
import functools

import jax
import jax.numpy as jnp
from jax import lax
from jax.experimental import pallas as pl
from jax.experimental.pallas import tpu as pltpu
from jax.sharding import PartitionSpec as P

heat_diffusion = 0.15
advection = 0.4
solute_diffusion = 0.05
segregation = 0.3
momentum_diffusion = 0.1
darcy_drag = 0.5
mushy_ratio = 1.0 / 3.0

MESH = pl.DeviceIdType.MESH
HIGHEST = lax.Precision.HIGHEST
HEAT, SOLUTE, SPEED = 0, 1, 2
PANEL = 8


def lateral_sum(field):
    lane = lax.broadcasted_iota(jnp.int32, field.shape, 2)
    last = field.shape[2] - 1
    left = jnp.where(lane == 0, field, pltpu.roll(field, 1, 2))
    right = jnp.where(lane == last, field, pltpu.roll(field, last, 2))
    return left + right


def laplacian(field):
    centre = field[1:-1]
    return field[2:] + field[:-2] + lateral_sum(centre) - 4.0 * centre


def advance_speed(speed, mushy):
    centre = speed[1:-1]
    return centre + momentum_diffusion * laplacian(speed) - darcy_drag * mushy[1:-1] * centre


def advance_pair(heat, solute, speed, mushy):
    temp = heat * (1.0 - mushy * (1.0 - mushy_ratio))
    drift = advection * speed[1:-1]
    new_heat = (
        heat[1:-1] + heat_diffusion * laplacian(temp) - drift * (heat[1:-1] - heat[:-2])
    )
    new_solute = (
        solute[1:-1]
        + solute_diffusion * laplacian(solute)
        - drift * (solute[1:-1] - solute[:-2])
        + segregation * mushy[1:-1] * (temp[1:-1] - solute[1:-1])
    )
    return new_heat, new_solute


def split(values):
    high = values.astype(jnp.bfloat16)
    low = (values - high.astype(jnp.float32)).astype(jnp.bfloat16)
    return high, low


def inverse_factor(matrix_ref):
    order = matrix_ref.shape[0]
    lane = lax.broadcasted_iota(jnp.int32, (PANEL, order), 1)
    sub = lax.broadcasted_iota(jnp.int32, (PANEL, order), 0)
    rows = lax.broadcasted_iota(jnp.int32, (order, order), 0)
    lanes = lax.broadcasted_iota(jnp.int32, (order, order), 1)

    def panel(block, carry):
        base = pl.multiple_of(block * PANEL, PANEL)
        here = matrix_ref[pl.ds(base, PANEL), :]
        cols = [
            jnp.broadcast_to(
                jnp.sum(jnp.where(lane == base + s, here, 0.0), axis=1, keepdims=True),
                (PANEL, order),
            )
            for s in range(PANEL)
        ]
        upper = jnp.where(lane >= base, here, 0.0)
        inverse = jnp.where(lane < base, here, jnp.where(lane == base + sub, 1.0, 0.0))
        diagonal = jnp.zeros((PANEL, order), jnp.float32)
        for s in range(PANEL):
            pivot = cols[s][s : s + 1]
            diagonal = jnp.where(sub == s, pivot, diagonal)
            factor = jnp.where(sub > s, cols[s] / pivot, 0.0)
            upper = upper - factor * upper[s : s + 1]
            inverse = inverse - factor * inverse[s : s + 1]
            for t in range(s + 1, PANEL):
                cols[t] = cols[t] - factor * cols[t][s : s + 1]
        scale = 1.0 / jnp.sqrt(diagonal)
        upper = upper * scale
        inverse = inverse * scale
        right = jnp.where(lane < base + PANEL, inverse, upper)
        change = lax.dot_general(
            upper, right, (((0,), (0,)), ((), ())),
            precision=HIGHEST, preferred_element_type=jnp.float32,
        )
        old = matrix_ref[...]
        kept = jnp.where((lanes >= base) & (lanes < base + PANEL), 0.0, old)
        matrix_ref[...] = jnp.where(rows >= base + PANEL, kept - change, old)
        matrix_ref[pl.ds(base, PANEL), :] = inverse
        return carry

    lax.fori_loop(0, order // PANEL, panel, 0)


def kernel(
    slabs, halves,
    hc_ref, v_ref, mask_ref, index_ref, value_ref, error_ref,
    out_hc_ref, out_v_ref,
    hc, vel, raw, mushy, own, other, seen, square,
    in_sem, out_sem, halo_send, halo_recv, state_send, state_recv, seen_send, seen_recv,
):
    members = own.shape[2]
    width = own.shape[3]
    depth = own.shape[1]
    groups = members // 8
    everyone = slabs * halves
    ens = members * halves
    slab = lax.axis_index("space")
    half = lax.axis_index("mem")
    me = slab * halves + half
    first = slab == 0
    last = slab == slabs - 1

    load_v = pltpu.make_async_copy(v_ref, vel, in_sem.at[0])
    load_hc = pltpu.make_async_copy(hc_ref, hc, in_sem.at[1])
    load_v.start()
    load_hc.start()

    barrier = pltpu.get_barrier_semaphore()

    def greet(step, carry):
        peer = lax.rem(me + step, everyone)
        pl.semaphore_signal(
            barrier, inc=1, device_id=(peer // halves, lax.rem(peer, halves)), device_id_type=MESH
        )
        return carry

    lax.fori_loop(1, everyone, greet, 0)

    for z in range(depth):
        row = mask_ref[z : z + 1, :].astype(jnp.float32)
        mushy[z + 2] = jnp.broadcast_to(row, (8, width))

    def relayout(zs):
        for z in zs:
            raw[HEAT, z + 2] = hc[pl.ds(z, members, stride=2 * depth), :]
            raw[SOLUTE, z + 2] = hc[pl.ds(depth + z, members, stride=2 * depth), :]
            raw[SPEED, z + 2] = vel[pl.ds(z, members, stride=depth), :]

    load_v.wait()
    load_hc.wait()
    relayout((0, 1, depth - 2, depth - 1))

    def halo(direction, source, target, to, part):
        ref = raw if part == 0 else mushy
        pick = (lambda r, a: r.at[:, pl.ds(a, 2)]) if part == 0 else (lambda r, a: r.at[pl.ds(a, 2)])
        return pltpu.make_async_remote_copy(
            src_ref=pick(ref, source),
            dst_ref=pick(ref, target),
            send_sem=halo_send.at[direction, part],
            recv_sem=halo_recv.at[direction, part],
            device_id=(to, half),
            device_id_type=MESH,
        )

    up = [halo(0, 2, depth + 2, lax.rem(slab + slabs - 1, slabs), part) for part in range(2)]
    down = [halo(1, depth, 0, lax.rem(slab + 1, slabs), part) for part in range(2)]

    @pl.when(first)
    def _():
        raw[:, 0:2] = jnp.zeros((3, 2, members, width), jnp.float32)
        mushy[0:2] = jnp.zeros((2, 8, width), jnp.float32)

    @pl.when(last)
    def _():
        raw[:, depth + 2 : depth + 4] = jnp.zeros((3, 2, members, width), jnp.float32)
        mushy[depth + 2 : depth + 4] = jnp.zeros((2, 8, width), jnp.float32)

    pl.semaphore_wait(barrier, everyone - 1)

    @pl.when(jnp.logical_not(first))
    def _():
        for copy in up:
            copy.start()

    @pl.when(jnp.logical_not(last))
    def _():
        for copy in down:
            copy.start()

    relayout(range(2, depth - 2))

    pieces = []

    def send(field, start, count):
        number = len(pieces)
        copies = []
        for hop in range(1, halves):
            copies.append(
                pltpu.make_async_remote_copy(
                    src_ref=own.at[field, pl.ds(start, count)],
                    dst_ref=other.at[hop - 1, field, pl.ds(start, count)],
                    send_sem=state_send.at[hop - 1, number],
                    recv_sem=state_recv.at[hop - 1, number],
                    device_id=(slab, lax.rem(half + hop, halves)),
                    device_id_type=MESH,
                )
            )
        for copy in copies:
            copy.start()
        pieces.append((field, start, count, copies))

    def inner_speed(group, carry):
        at = pl.ds(pl.multiple_of(group * 8, 8), 8)
        mask = mushy[2 : depth + 2]
        speed = advance_speed(raw[SPEED, 2 : depth + 2, at, :], mask)
        own[SPEED, 2 : depth - 2, at, :] = advance_speed(speed, mask[1:-1])
        return carry

    lax.fori_loop(0, groups, inner_speed, 0)
    middle = depth // 2
    send(SPEED, 2, middle - 2)
    send(SPEED, middle, middle - 2)

    def inner_pair(group, carry):
        at = pl.ds(pl.multiple_of(group * 8, 8), 8)
        mask = mushy[2 : depth + 2]
        before = raw[SPEED, 2 : depth + 2, at, :]
        heat, solute = advance_pair(
            raw[HEAT, 2 : depth + 2, at, :], raw[SOLUTE, 2 : depth + 2, at, :], before, mask
        )
        heat, solute = advance_pair(heat, solute, advance_speed(before, mask), mask[1:-1])
        own[HEAT, 2 : depth - 2, at, :] = heat
        own[SOLUTE, 2 : depth - 2, at, :] = solute
        return carry

    lax.fori_loop(0, groups, inner_pair, 0)
    send(HEAT, 2, middle - 2)
    send(HEAT, middle, middle - 2)

    @pl.when(jnp.logical_not(last))
    def _():
        for copy in up:
            copy.wait_recv()

    @pl.when(jnp.logical_not(first))
    def _():
        for copy in down:
            copy.wait_recv()

    def edges(group, carry):
        at = pl.ds(pl.multiple_of(group * 8, 8), 8)
        for begin, outside, edge in ((0, first, 0), (depth - 2, last, 3)):
            mask = mushy[begin : begin + 6]
            before = raw[SPEED, begin : begin + 6, at, :]
            heat, solute = advance_pair(
                raw[HEAT, begin : begin + 6, at, :], raw[SOLUTE, begin : begin + 6, at, :], before, mask
            )
            speed = advance_speed(before, mask)
            row = lax.broadcasted_iota(jnp.int32, heat.shape, 0)
            beyond = jnp.logical_and(row == edge, outside)
            heat, solute, speed = [jnp.where(beyond, 0.0, q) for q in (heat, solute, speed)]
            mask = mask[1:-1]
            new_heat, new_solute = advance_pair(heat, solute, speed, mask)
            own[HEAT, begin : begin + 2, at, :] = new_heat
            own[SOLUTE, begin : begin + 2, at, :] = new_solute
            own[SPEED, begin : begin + 2, at, :] = advance_speed(speed, mask)
        return carry

    lax.fori_loop(0, groups, edges, 0)

    lane = lax.broadcasted_iota(jnp.int32, (members, width), 1)
    per_slab = index_ref.shape[0]
    observed = jnp.zeros((members, width), jnp.float32)
    value = jnp.zeros((members, width), jnp.float32)
    error = jnp.ones((members, width), jnp.float32)
    for o in range(per_slab):
        cell = index_ref[o]
        z = cell // width
        w = cell - z * width
        factor = 1.0 - mushy[z + 2][0:1] * (1.0 - mushy_ratio)
        temp = jnp.where(lane == w, own[HEAT, z] * factor, 0.0)
        observed = jnp.where(lane == o, jnp.sum(temp, axis=1, keepdims=True), observed)
        value = jnp.where(lane == o, value_ref[o], value)
        error = jnp.where(lane == o, error_ref[o], error)
    square[...] = jnp.zeros((ens, width), jnp.float32)
    square[pl.ds(pl.multiple_of(half * members, 8), members), :] = (observed - value) / error
    turned = square[...].T
    seen[me] = turned[0:8] + pltpu.roll(turned[8:16], ens // 2, 1)

    def tell_copy(peer):
        return pltpu.make_async_remote_copy(
            src_ref=seen.at[me],
            dst_ref=seen.at[me],
            send_sem=seen_send.at[0],
            recv_sem=seen_recv.at[0],
            device_id=(peer // halves, lax.rem(peer, halves)),
            device_id_type=MESH,
        )

    def tell(step, carry):
        tell_copy(lax.rem(me + step, everyone)).start()
        return carry

    lax.fori_loop(1, everyone, tell, 0)

    for field in range(3):
        send(field, 0, 2)
        send(field, depth - 2, 2)
    send(SOLUTE, 2, middle - 2)
    send(SOLUTE, middle, middle - 2)

    rest = seen.at[pl.ds(0, everyone - 1)]
    pltpu.make_async_copy(rest, rest, seen_recv.at[0]).wait()

    got = seen[...].reshape(slabs, halves, 8, ens)
    place = lax.broadcasted_iota(jnp.int32, (slabs, 8, ens), 2)
    low = jnp.zeros((slabs, 8, ens), jnp.float32)
    high = jnp.zeros((slabs, 8, ens), jnp.float32)
    for m in range(halves):
        mine = (place >= m * members) & (place < (m + 1) * members)
        low = jnp.where(mine, got[:, m], low)
        high = jnp.where(mine, pltpu.roll(got[:, m], ens // 2, 2), high)
    deviation = jnp.concatenate(
        [low.reshape(slabs * 8, ens), high.reshape(slabs * 8, ens)], axis=0
    )
    mean = jnp.sum(deviation, axis=1, keepdims=True) * (1.0 / ens)
    root = 1.0 / (ens - 1.0) ** 0.5
    spread = (deviation - mean) * root
    project = -jnp.sum(spread * mean, axis=0, keepdims=True)
    gram = lax.dot_general(
        spread, spread, (((0,), (0,)), ((), ())),
        precision=HIGHEST, preferred_element_type=jnp.float32,
    )
    rows = lax.broadcasted_iota(jnp.int32, (ens, ens), 0)
    lanes = lax.broadcasted_iota(jnp.int32, (ens, ens), 1)
    square[...] = jnp.where(rows == lanes, 1.0, 0.0) + gram
    inverse_factor(square)
    inverse = square[...]
    shift = jnp.sum(inverse * project, axis=1, keepdims=True)
    shift = jnp.sum(inverse * shift, axis=0, keepdims=True)
    combined = inverse + shift * root
    combined = combined - jnp.sum(combined, axis=1, keepdims=True) * (1.0 / ens) + 1.0 / ens
    square[...] = pltpu.roll(combined, lax.rem(ens - half * members, ens), 1)
    weight_high, weight_low = split(square[pl.ds(pl.multiple_of(half * members, 8), members), :])
    weights = jnp.concatenate([weight_high, weight_high, weight_low], axis=1)

    for field, start, count, copies in pieces:
        for copy in copies:
            copy.wait_recv()
        for z in range(start, start + count, 2):
            parts = []
            for d in (z, z + 1):
                blocks = [own[field, d]] + [
                    other[halves - q - 1, field, d] for q in range(1, halves)
                ]
                parts.append(jnp.concatenate(blocks, axis=0))
            state_high, state_low = split(jnp.concatenate(parts, axis=1))
            mixed = jnp.dot(
                weights,
                jnp.concatenate([state_high, state_low, state_high], axis=0),
                preferred_element_type=jnp.float32,
            )
            for i, d in enumerate((z, z + 1)):
                block = mixed[:, i * width : (i + 1) * width]
                if field == SPEED:
                    vel[pl.ds(d, members, stride=depth), :] = block
                else:
                    hc[pl.ds(field * depth + d, members, stride=2 * depth), :] = block

    store_v = pltpu.make_async_copy(vel, out_v_ref, out_sem.at[0])
    store_hc = pltpu.make_async_copy(hc, out_hc_ref, out_sem.at[1])
    store_v.start()
    store_hc.start()

    for _, _, _, copies in pieces:
        for copy in copies:
            copy.wait_send()
    pltpu.make_async_copy(rest, rest, seen_send.at[0]).wait()

    @pl.when(jnp.logical_not(first))
    def _():
        for copy in up:
            copy.wait_send()

    @pl.when(jnp.logical_not(last))
    def _():
        for copy in down:
            copy.wait_send()

    store_v.wait()
    store_hc.wait()


def on_device(slabs, halves, member_heat_solute, velocity, phase_mask, obs_index, obs_value, obs_error):
    members, _, depth, width = member_heat_solute.shape
    ens = members * halves
    vmem = pl.BlockSpec(memory_space=pltpu.VMEM)
    smem = pl.BlockSpec(memory_space=pltpu.SMEM)
    anywhere = pl.BlockSpec(memory_space=pl.ANY)
    hc, vel = pl.pallas_call(
        functools.partial(kernel, slabs, halves),
        out_shape=(
            jax.ShapeDtypeStruct((members * 2 * depth, width), jnp.float32),
            jax.ShapeDtypeStruct((members * depth, width), jnp.float32),
        ),
        in_specs=[anywhere, anywhere, vmem, smem, smem, smem],
        out_specs=(anywhere, anywhere),
        scratch_shapes=[
            pltpu.VMEM((members * 2 * depth, width), jnp.float32),
            pltpu.VMEM((members * depth, width), jnp.float32),
            pltpu.VMEM((3, depth + 4, members, width), jnp.float32),
            pltpu.VMEM((depth + 4, 8, width), jnp.float32),
            pltpu.VMEM((3, depth, members, width), jnp.float32),
            pltpu.VMEM((halves - 1, 3, depth, members, width), jnp.float32),
            pltpu.VMEM((slabs * halves, 8, ens), jnp.float32),
            pltpu.VMEM((ens, ens), jnp.float32),
            pltpu.SemaphoreType.DMA((2,)),
            pltpu.SemaphoreType.DMA((2,)),
            pltpu.SemaphoreType.DMA((2, 2)),
            pltpu.SemaphoreType.DMA((2, 2)),
            pltpu.SemaphoreType.DMA((halves - 1, 12)),
            pltpu.SemaphoreType.DMA((halves - 1, 12)),
            pltpu.SemaphoreType.DMA((1,)),
            pltpu.SemaphoreType.DMA((1,)),
        ],
        compiler_params=pltpu.CompilerParams(
            collective_id=0, has_side_effects=True, vmem_limit_bytes=48 * 1024 * 1024
        ),
    )(
        member_heat_solute.reshape(-1, width),
        velocity.reshape(-1, width),
        phase_mask,
        obs_index,
        obs_value,
        obs_error,
    )
    return hc.reshape(members, 2, depth, width), vel.reshape(members, depth, width)


def solution(mesh):
    return jax.shard_map(
        functools.partial(on_device, mesh.shape["space"], mesh.shape["mem"]),
        mesh=mesh,
        in_specs=(
            P("mem", None, "space", None),
            P("mem", "space", None),
            P("space", None),
            P("space"),
            P("space"),
            P("space"),
        ),
        out_specs=(P("mem", None, "space", None), P("mem", "space", None)),
        check_vma=False,
    )
```

```python
import functools

import jax
import jax.numpy as jnp
from jax import lax
from jax.experimental import pallas as pl
from jax.experimental.pallas import tpu as pltpu
from jax.sharding import PartitionSpec as P

heat_diffusion = 0.15
advection = 0.4
solute_diffusion = 0.05
segregation = 0.3
momentum_diffusion = 0.1
darcy_drag = 0.5
mushy_ratio = 1.0 / 3.0

MESH = pl.DeviceIdType.MESH
HIGHEST = lax.Precision.HIGHEST
HEAT, SOLUTE, SPEED = 0, 1, 2
PANEL = 8


def lateral_sum(field):
    lane = lax.broadcasted_iota(jnp.int32, field.shape, 2)
    last = field.shape[2] - 1
    left = jnp.where(lane == 0, field, pltpu.roll(field, 1, 2))
    right = jnp.where(lane == last, field, pltpu.roll(field, last, 2))
    return left + right


def laplacian(field):
    centre = field[1:-1]
    return field[2:] + field[:-2] + lateral_sum(centre) - 4.0 * centre


def advance_speed(speed, mushy):
    centre = speed[1:-1]
    return centre + momentum_diffusion * laplacian(speed) - darcy_drag * mushy[1:-1] * centre


def advance_pair(heat, solute, speed, mushy):
    temp = heat * (1.0 - mushy * (1.0 - mushy_ratio))
    drift = advection * speed[1:-1]
    new_heat = (
        heat[1:-1] + heat_diffusion * laplacian(temp) - drift * (heat[1:-1] - heat[:-2])
    )
    new_solute = (
        solute[1:-1]
        + solute_diffusion * laplacian(solute)
        - drift * (solute[1:-1] - solute[:-2])
        + segregation * mushy[1:-1] * (temp[1:-1] - solute[1:-1])
    )
    return new_heat, new_solute


def split(values):
    high = values.astype(jnp.bfloat16)
    low = (values - high.astype(jnp.float32)).astype(jnp.bfloat16)
    return high, low


def inverse_factor(matrix_ref):
    order = matrix_ref.shape[0]
    lane = lax.broadcasted_iota(jnp.int32, (PANEL, order), 1)
    sub = lax.broadcasted_iota(jnp.int32, (PANEL, order), 0)
    rows = lax.broadcasted_iota(jnp.int32, (order, order), 0)
    lanes = lax.broadcasted_iota(jnp.int32, (order, order), 1)

    def panel(block, carry):
        base = pl.multiple_of(block * PANEL, PANEL)
        here = matrix_ref[pl.ds(base, PANEL), :]
        cols = [
            jnp.broadcast_to(
                jnp.sum(jnp.where(lane == base + s, here, 0.0), axis=1, keepdims=True),
                (PANEL, order),
            )
            for s in range(PANEL)
        ]
        upper = jnp.where(lane >= base, here, 0.0)
        inverse = jnp.where(lane < base, here, jnp.where(lane == base + sub, 1.0, 0.0))
        diagonal = jnp.zeros((PANEL, order), jnp.float32)
        for s in range(PANEL):
            pivot = cols[s][s : s + 1]
            diagonal = jnp.where(sub == s, pivot, diagonal)
            factor = jnp.where(sub > s, cols[s] / pivot, 0.0)
            upper = upper - factor * upper[s : s + 1]
            inverse = inverse - factor * inverse[s : s + 1]
            for t in range(s + 1, PANEL):
                cols[t] = cols[t] - factor * cols[t][s : s + 1]
        scale = 1.0 / jnp.sqrt(diagonal)
        upper = upper * scale
        inverse = inverse * scale
        right = jnp.where(lane < base + PANEL, inverse, upper)
        change = lax.dot_general(
            upper, right, (((0,), (0,)), ((), ())),
            precision=HIGHEST, preferred_element_type=jnp.float32,
        )
        old = matrix_ref[...]
        kept = jnp.where((lanes >= base) & (lanes < base + PANEL), 0.0, old)
        matrix_ref[...] = jnp.where(rows >= base + PANEL, kept - change, old)
        matrix_ref[pl.ds(base, PANEL), :] = inverse
        return carry

    lax.fori_loop(0, order // PANEL, panel, 0)


def kernel(
    slabs, halves,
    hc_ref, v_ref, phase_ref, cell_ref, datum_ref, deviate_ref,
    out_hc_ref, out_v_ref,
    mask_ref, index_ref, value_ref, error_ref, hc, vel, raw, mushy, own, other, seen, square,
    in_sem, out_sem, halo_send, halo_recv, state_send, state_recv, seen_send, seen_recv,
):
    members = own.shape[2]
    width = own.shape[3]
    depth = own.shape[1]
    groups = members // 8
    everyone = slabs * halves
    ens = members * halves
    slab = lax.axis_index("space")
    half = lax.axis_index("mem")
    me = slab * halves + half
    first = slab == 0
    last = slab == slabs - 1

    load_v = pltpu.make_async_copy(v_ref, vel, in_sem.at[0])
    load_hc = pltpu.make_async_copy(hc_ref, hc, in_sem.at[1])
    load_mask = pltpu.make_async_copy(phase_ref, mask_ref, in_sem.at[2])
    load_observed = [
        pltpu.make_async_copy(cell_ref, index_ref, in_sem.at[3]),
        pltpu.make_async_copy(datum_ref, value_ref, in_sem.at[4]),
        pltpu.make_async_copy(deviate_ref, error_ref, in_sem.at[5]),
    ]
    load_mask.start()
    load_v.start()
    load_hc.start()
    for load in load_observed:
        load.start()

    barrier = pltpu.get_barrier_semaphore()

    def greet(step, carry):
        peer = lax.rem(me + step, everyone)
        pl.semaphore_signal(
            barrier, inc=1, device_id=(peer // halves, lax.rem(peer, halves)), device_id_type=MESH
        )
        return carry

    lax.fori_loop(1, everyone, greet, 0)

    load_mask.wait()
    for z in range(depth):
        row = mask_ref[z : z + 1, :].astype(jnp.float32)
        mushy[z + 2] = jnp.broadcast_to(row, (8, width))

    def relayout_speed(zs):
        for z in zs:
            raw[SPEED, z + 2] = vel[pl.ds(z, members, stride=depth), :]

    def relayout_pair(zs):
        for z in zs:
            raw[HEAT, z + 2] = hc[pl.ds(z, members, stride=2 * depth), :]
            raw[SOLUTE, z + 2] = hc[pl.ds(depth + z, members, stride=2 * depth), :]

    load_v.wait()
    relayout_speed(range(depth))

    def inner_speed(group, carry):
        at = pl.ds(pl.multiple_of(group * 8, 8), 8)
        mask = mushy[2 : depth + 2]
        speed = advance_speed(raw[SPEED, 2 : depth + 2, at, :], mask)
        own[SPEED, 2 : depth - 2, at, :] = advance_speed(speed, mask[1:-1])
        return carry

    lax.fori_loop(0, groups, inner_speed, 0)
    load_hc.wait()
    relayout_pair((0, 1, depth - 2, depth - 1))

    def halo(direction, source, target, to, part):
        ref = raw if part == 0 else mushy
        pick = (lambda r, a: r.at[:, pl.ds(a, 2)]) if part == 0 else (lambda r, a: r.at[pl.ds(a, 2)])
        return pltpu.make_async_remote_copy(
            src_ref=pick(ref, source),
            dst_ref=pick(ref, target),
            send_sem=halo_send.at[direction, part],
            recv_sem=halo_recv.at[direction, part],
            device_id=(to, half),
            device_id_type=MESH,
        )

    up = [halo(0, 2, depth + 2, lax.rem(slab + slabs - 1, slabs), part) for part in range(2)]
    down = [halo(1, depth, 0, lax.rem(slab + 1, slabs), part) for part in range(2)]

    @pl.when(first)
    def _():
        raw[:, 0:2] = jnp.zeros((3, 2, members, width), jnp.float32)
        mushy[0:2] = jnp.zeros((2, 8, width), jnp.float32)

    @pl.when(last)
    def _():
        raw[:, depth + 2 : depth + 4] = jnp.zeros((3, 2, members, width), jnp.float32)
        mushy[depth + 2 : depth + 4] = jnp.zeros((2, 8, width), jnp.float32)

    pl.semaphore_wait(barrier, everyone - 1)

    @pl.when(jnp.logical_not(first))
    def _():
        for copy in up:
            copy.start()

    @pl.when(jnp.logical_not(last))
    def _():
        for copy in down:
            copy.start()

    pieces = []

    def send(field, start, count):
        number = len(pieces)
        copies = []
        for hop in range(1, halves):
            copies.append(
                pltpu.make_async_remote_copy(
                    src_ref=own.at[field, pl.ds(start, count)],
                    dst_ref=other.at[hop - 1, field, pl.ds(start, count)],
                    send_sem=state_send.at[hop - 1, number],
                    recv_sem=state_recv.at[hop - 1, number],
                    device_id=(slab, lax.rem(half + hop, halves)),
                    device_id_type=MESH,
                )
            )
        for copy in copies:
            copy.start()
        pieces.append((field, start, count, copies))

    middle = depth // 2
    send(SPEED, 2, middle - 2)
    send(SPEED, middle, middle - 2)
    relayout_pair(range(2, depth - 2))

    def inner_pair(group, carry):
        at = pl.ds(pl.multiple_of(group * 8, 8), 8)
        mask = mushy[2 : depth + 2]
        before = raw[SPEED, 2 : depth + 2, at, :]
        heat, solute = advance_pair(
            raw[HEAT, 2 : depth + 2, at, :], raw[SOLUTE, 2 : depth + 2, at, :], before, mask
        )
        heat, solute = advance_pair(heat, solute, advance_speed(before, mask), mask[1:-1])
        own[HEAT, 2 : depth - 2, at, :] = heat
        own[SOLUTE, 2 : depth - 2, at, :] = solute
        return carry

    lax.fori_loop(0, groups, inner_pair, 0)

    @pl.when(jnp.logical_not(last))
    def _():
        for copy in up:
            copy.wait_recv()

    @pl.when(jnp.logical_not(first))
    def _():
        for copy in down:
            copy.wait_recv()

    def edges(group, carry):
        at = pl.ds(pl.multiple_of(group * 8, 8), 8)
        for begin, outside, edge in ((0, first, 0), (depth - 2, last, 3)):
            mask = mushy[begin : begin + 6]
            before = raw[SPEED, begin : begin + 6, at, :]
            heat, solute = advance_pair(
                raw[HEAT, begin : begin + 6, at, :], raw[SOLUTE, begin : begin + 6, at, :], before, mask
            )
            speed = advance_speed(before, mask)
            row = lax.broadcasted_iota(jnp.int32, heat.shape, 0)
            beyond = jnp.logical_and(row == edge, outside)
            heat, solute, speed = [jnp.where(beyond, 0.0, q) for q in (heat, solute, speed)]
            mask = mask[1:-1]
            new_heat, new_solute = advance_pair(heat, solute, speed, mask)
            own[HEAT, begin : begin + 2, at, :] = new_heat
            own[SOLUTE, begin : begin + 2, at, :] = new_solute
            own[SPEED, begin : begin + 2, at, :] = advance_speed(speed, mask)
        return carry

    lax.fori_loop(0, groups, edges, 0)

    lane = lax.broadcasted_iota(jnp.int32, (members, width), 1)
    per_slab = index_ref.shape[0]
    for load in load_observed:
        load.wait()
    observed = jnp.zeros((members, width), jnp.float32)
    value = jnp.zeros((members, width), jnp.float32)
    error = jnp.ones((members, width), jnp.float32)
    for o in range(per_slab):
        cell = index_ref[o]
        z = cell // width
        w = cell - z * width
        factor = 1.0 - mushy[z + 2][0:1] * (1.0 - mushy_ratio)
        temp = jnp.where(lane == w, own[HEAT, z] * factor, 0.0)
        observed = jnp.where(lane == o, jnp.sum(temp, axis=1, keepdims=True), observed)
        value = jnp.where(lane == o, value_ref[o], value)
        error = jnp.where(lane == o, error_ref[o], error)
    square[...] = jnp.zeros((ens, width), jnp.float32)
    square[pl.ds(pl.multiple_of(half * members, 8), members), :] = (observed - value) / error
    turned = square[...].T
    seen[me] = turned[0:8] + pltpu.roll(turned[8:16], ens // 2, 1)

    def tell_copy(peer):
        return pltpu.make_async_remote_copy(
            src_ref=seen.at[me],
            dst_ref=seen.at[me],
            send_sem=seen_send.at[0],
            recv_sem=seen_recv.at[0],
            device_id=(peer // halves, lax.rem(peer, halves)),
            device_id_type=MESH,
        )

    def tell(step, carry):
        tell_copy(lax.rem(me + step, everyone)).start()
        return carry

    lax.fori_loop(1, everyone, tell, 0)

    for field in (SPEED, HEAT, SOLUTE):
        send(field, 0, 2)
        send(field, depth - 2, 2)
        if field != SPEED:
            send(field, 2, middle - 2)
            send(field, middle, middle - 2)

    rest = seen.at[pl.ds(0, everyone - 1)]
    pltpu.make_async_copy(rest, rest, seen_recv.at[0]).wait()

    got = seen[...].reshape(slabs, halves, 8, ens)
    place = lax.broadcasted_iota(jnp.int32, (slabs, 8, ens), 2)
    low = jnp.zeros((slabs, 8, ens), jnp.float32)
    high = jnp.zeros((slabs, 8, ens), jnp.float32)
    for m in range(halves):
        mine = (place >= m * members) & (place < (m + 1) * members)
        low = jnp.where(mine, got[:, m], low)
        high = jnp.where(mine, pltpu.roll(got[:, m], ens // 2, 2), high)
    deviation = jnp.concatenate(
        [low.reshape(slabs * 8, ens), high.reshape(slabs * 8, ens)], axis=0
    )
    mean = jnp.sum(deviation, axis=1, keepdims=True) * (1.0 / ens)
    root = 1.0 / (ens - 1.0) ** 0.5
    spread = (deviation - mean) * root
    project = -jnp.sum(spread * mean, axis=0, keepdims=True)
    gram = lax.dot_general(
        spread, spread, (((0,), (0,)), ((), ())),
        precision=HIGHEST, preferred_element_type=jnp.float32,
    )
    rows = lax.broadcasted_iota(jnp.int32, (ens, ens), 0)
    lanes = lax.broadcasted_iota(jnp.int32, (ens, ens), 1)
    square[...] = jnp.where(rows == lanes, 1.0, 0.0) + gram
    inverse_factor(square)
    inverse = square[...]
    shift = jnp.sum(inverse * project, axis=1, keepdims=True)
    shift = jnp.sum(inverse * shift, axis=0, keepdims=True)
    combined = inverse + shift * root
    combined = combined - jnp.sum(combined, axis=1, keepdims=True) * (1.0 / ens) + 1.0 / ens
    square[...] = pltpu.roll(combined, lax.rem(ens - half * members, ens), 1)
    weight_high, weight_low = split(square[pl.ds(pl.multiple_of(half * members, 8), members), :])
    weights = jnp.concatenate([weight_high, weight_high, weight_low], axis=1)

    store_v = pltpu.make_async_copy(vel, out_v_ref, out_sem.at[0])
    store_hc = pltpu.make_async_copy(hc, out_hc_ref, out_sem.at[1])
    for field, start, count, copies in pieces:
        if field == HEAT and start == 0:
            store_v.start()
        for copy in copies:
            copy.wait_recv()
        for z in range(start, start + count, 2):
            parts = []
            for d in (z, z + 1):
                blocks = [own[field, d]] + [
                    other[halves - q - 1, field, d] for q in range(1, halves)
                ]
                parts.append(jnp.concatenate(blocks, axis=0))
            state_high, state_low = split(jnp.concatenate(parts, axis=1))
            mixed = jnp.dot(
                weights,
                jnp.concatenate([state_high, state_low, state_high], axis=0),
                preferred_element_type=jnp.float32,
            )
            for i, d in enumerate((z, z + 1)):
                block = mixed[:, i * width : (i + 1) * width]
                if field == SPEED:
                    vel[pl.ds(d, members, stride=depth), :] = block
                else:
                    hc[pl.ds(field * depth + d, members, stride=2 * depth), :] = block

    store_hc.start()

    for _, _, _, copies in pieces:
        for copy in copies:
            copy.wait_send()
    pltpu.make_async_copy(rest, rest, seen_send.at[0]).wait()

    @pl.when(jnp.logical_not(first))
    def _():
        for copy in up:
            copy.wait_send()

    @pl.when(jnp.logical_not(last))
    def _():
        for copy in down:
            copy.wait_send()

    store_v.wait()
    store_hc.wait()


def on_device(slabs, halves, member_heat_solute, velocity, phase_mask, obs_index, obs_value, obs_error):
    members, _, depth, width = member_heat_solute.shape
    ens = members * halves
    anywhere = pl.BlockSpec(memory_space=pltpu.HBM)
    hc, vel = pl.pallas_call(
        functools.partial(kernel, slabs, halves),
        out_shape=(
            jax.ShapeDtypeStruct((members * 2 * depth, width), jnp.float32),
            jax.ShapeDtypeStruct((members * depth, width), jnp.float32),
        ),
        in_specs=[anywhere] * 6,
        out_specs=(anywhere, anywhere),
        scratch_shapes=[
            pltpu.VMEM((depth, width), jnp.int32),
            pltpu.SMEM(obs_index.shape, jnp.int32),
            pltpu.SMEM(obs_value.shape, jnp.float32),
            pltpu.SMEM(obs_error.shape, jnp.float32),
            pltpu.VMEM((members * 2 * depth, width), jnp.float32),
            pltpu.VMEM((members * depth, width), jnp.float32),
            pltpu.VMEM((3, depth + 4, members, width), jnp.float32),
            pltpu.VMEM((depth + 4, 8, width), jnp.float32),
            pltpu.VMEM((3, depth, members, width), jnp.float32),
            pltpu.VMEM((halves - 1, 3, depth, members, width), jnp.float32),
            pltpu.VMEM((slabs * halves, 8, ens), jnp.float32),
            pltpu.VMEM((ens, ens), jnp.float32),
            pltpu.SemaphoreType.DMA((6,)),
            pltpu.SemaphoreType.DMA((2,)),
            pltpu.SemaphoreType.DMA((2, 2)),
            pltpu.SemaphoreType.DMA((2, 2)),
            pltpu.SemaphoreType.DMA((halves - 1, 12)),
            pltpu.SemaphoreType.DMA((halves - 1, 12)),
            pltpu.SemaphoreType.DMA((1,)),
            pltpu.SemaphoreType.DMA((1,)),
        ],
        compiler_params=pltpu.CompilerParams(
            collective_id=0, has_side_effects=True, vmem_limit_bytes=62 * 1024 * 1024
        ),
    )(
        member_heat_solute.reshape(-1, width),
        velocity.reshape(-1, width),
        phase_mask,
        obs_index,
        obs_value,
        obs_error,
    )
    return hc.reshape(members, 2, depth, width), vel.reshape(members, depth, width)


def solution(mesh):
    return jax.shard_map(
        functools.partial(on_device, mesh.shape["space"], mesh.shape["mem"]),
        mesh=mesh,
        in_specs=(
            P("mem", None, "space", None),
            P("mem", "space", None),
            P("space", None),
            P("space"),
            P("space"),
            P("space"),
        ),
        out_specs=(P("mem", None, "space", None), P("mem", "space", None)),
        check_vma=False,
    )
```

```python
import functools

import jax
import jax.numpy as jnp
from jax import lax
from jax.experimental import pallas as pl
from jax.experimental.pallas import tpu as pltpu
from jax.sharding import PartitionSpec as P

heat_diffusion = 0.15
advection = 0.4
solute_diffusion = 0.05
segregation = 0.3
momentum_diffusion = 0.1
darcy_drag = 0.5
mushy_ratio = 1.0 / 3.0

MESH = pl.DeviceIdType.MESH
HIGHEST = lax.Precision.HIGHEST
HEAT, SOLUTE, SPEED = 0, 1, 2
PANEL = 16


def lateral_sum(field):
    lane = lax.broadcasted_iota(jnp.int32, field.shape, 2)
    last = field.shape[2] - 1
    left = jnp.where(lane == 0, field, pltpu.roll(field, 1, 2))
    right = jnp.where(lane == last, field, pltpu.roll(field, last, 2))
    return left + right


def laplacian(field):
    centre = field[1:-1]
    return field[2:] + field[:-2] + lateral_sum(centre) - 4.0 * centre


def advance_speed(speed, mushy):
    centre = speed[1:-1]
    return centre + momentum_diffusion * laplacian(speed) - darcy_drag * mushy[1:-1] * centre


def advance_pair(heat, solute, speed, mushy):
    temp = heat * (1.0 - mushy * (1.0 - mushy_ratio))
    drift = advection * speed[1:-1]
    new_heat = (
        heat[1:-1] + heat_diffusion * laplacian(temp) - drift * (heat[1:-1] - heat[:-2])
    )
    new_solute = (
        solute[1:-1]
        + solute_diffusion * laplacian(solute)
        - drift * (solute[1:-1] - solute[:-2])
        + segregation * mushy[1:-1] * (temp[1:-1] - solute[1:-1])
    )
    return new_heat, new_solute


def split(values):
    high = values.astype(jnp.bfloat16)
    low = (values - high.astype(jnp.float32)).astype(jnp.bfloat16)
    return high, low


def split_three(values):
    parts = []
    for _ in range(3):
        part = values.astype(jnp.bfloat16).astype(jnp.float32)
        parts.append(part)
        values = values - part
    return parts


def inverse_factor(matrix_ref):
    order = matrix_ref.shape[0]
    lane = lax.broadcasted_iota(jnp.int32, (PANEL, order), 1)
    sub = lax.broadcasted_iota(jnp.int32, (PANEL, order), 0)
    rows = lax.broadcasted_iota(jnp.int32, (order, order), 0)
    lanes = lax.broadcasted_iota(jnp.int32, (order, order), 1)

    def panel(block, carry):
        base = pl.multiple_of(block * PANEL, PANEL)
        here = matrix_ref[pl.ds(base, PANEL), :]
        cols = [
            jnp.broadcast_to(
                jnp.sum(jnp.where(lane == base + s, here, 0.0), axis=1, keepdims=True),
                (PANEL, order),
            )
            for s in range(PANEL)
        ]
        upper = jnp.where(lane >= base, here, 0.0)
        inverse = jnp.where(lane < base, here, jnp.where(lane == base + sub, 1.0, 0.0))
        diagonal = jnp.zeros((PANEL, order), jnp.float32)
        for s in range(PANEL):
            pivot = cols[s][s : s + 1]
            diagonal = jnp.where(sub == s, pivot, diagonal)
            factor = jnp.where(sub > s, cols[s] / pivot, 0.0)
            upper = upper - factor * upper[s : s + 1]
            inverse = inverse - factor * inverse[s : s + 1]
            for t in range(s + 1, PANEL):
                cols[t] = cols[t] - factor * cols[t][s : s + 1]
        scale = 1.0 / jnp.sqrt(diagonal)
        upper = upper * scale
        inverse = inverse * scale
        right = jnp.where(lane < base + PANEL, inverse, upper)
        upper_parts = split_three(upper)
        right_parts = split_three(right)
        change = lax.dot_general(
            jnp.concatenate([upper_parts[i] for i in (0, 0, 1, 1, 0, 2)], axis=0).astype(jnp.bfloat16),
            jnp.concatenate([right_parts[i] for i in (0, 1, 0, 1, 2, 0)], axis=0).astype(jnp.bfloat16),
            (((0,), (0,)), ((), ())),
            preferred_element_type=jnp.float32,
        )
        old = matrix_ref[...]
        kept = jnp.where((lanes >= base) & (lanes < base + PANEL), 0.0, old)
        matrix_ref[...] = jnp.where(rows >= base + PANEL, kept - change, old)
        matrix_ref[pl.ds(base, PANEL), :] = inverse
        return carry

    lax.fori_loop(0, order // PANEL, panel, 0)


def kernel(
    slabs, halves,
    hc_ref, v_ref, phase_ref, cell_ref, datum_ref, deviate_ref,
    out_hc_ref, out_v_ref,
    mask_ref, index_ref, value_ref, error_ref, hc, vel, raw, mushy, own, other, seen, square,
    in_sem, halo_send, halo_recv, state_send, state_recv, seen_send, seen_recv,
):
    members = own.shape[2]
    width = own.shape[3]
    depth = own.shape[1]
    groups = members // 8
    everyone = slabs * halves
    ens = members * halves
    slab = lax.axis_index("space")
    half = lax.axis_index("mem")
    me = slab * halves + half
    first = slab == 0
    last = slab == slabs - 1

    load_v = pltpu.make_async_copy(v_ref, vel, in_sem.at[0])
    load_hc = pltpu.make_async_copy(hc_ref, hc, in_sem.at[1])
    load_mask = pltpu.make_async_copy(phase_ref, mask_ref, in_sem.at[2])
    load_observed = [
        pltpu.make_async_copy(cell_ref, index_ref, in_sem.at[3]),
        pltpu.make_async_copy(datum_ref, value_ref, in_sem.at[4]),
        pltpu.make_async_copy(deviate_ref, error_ref, in_sem.at[5]),
    ]
    load_mask.start()
    load_v.start()
    load_hc.start()
    for load in load_observed:
        load.start()

    barrier = pltpu.get_barrier_semaphore()

    def greet(step, carry):
        peer = lax.rem(me + step, everyone)
        pl.semaphore_signal(
            barrier, inc=1, device_id=(peer // halves, lax.rem(peer, halves)), device_id_type=MESH
        )
        return carry

    lax.fori_loop(1, everyone, greet, 0)

    load_mask.wait()
    for z in range(depth):
        row = mask_ref[z : z + 1, :].astype(jnp.float32)
        mushy[z + 2] = jnp.broadcast_to(row, (8, width))

    def relayout_speed(zs):
        for z in zs:
            raw[SPEED, z + 2] = vel[pl.ds(z, members, stride=depth), :]

    def relayout_pair(zs):
        for z in zs:
            raw[HEAT, z + 2] = hc[pl.ds(z, members, stride=2 * depth), :]
            raw[SOLUTE, z + 2] = hc[pl.ds(depth + z, members, stride=2 * depth), :]

    load_v.wait()
    relayout_speed(range(depth))

    def inner_speed(group, carry):
        at = pl.ds(pl.multiple_of(group * 8, 8), 8)
        mask = mushy[2 : depth + 2]
        speed = advance_speed(raw[SPEED, 2 : depth + 2, at, :], mask)
        own[SPEED, 2 : depth - 2, at, :] = advance_speed(speed, mask[1:-1])
        return carry

    lax.fori_loop(0, groups, inner_speed, 0)
    load_hc.wait()
    relayout_pair((0, 1, depth - 2, depth - 1))

    def halo(direction, source, target, to, part):
        ref = raw if part == 0 else mushy
        pick = (lambda r, a: r.at[:, pl.ds(a, 2)]) if part == 0 else (lambda r, a: r.at[pl.ds(a, 2)])
        return pltpu.make_async_remote_copy(
            src_ref=pick(ref, source),
            dst_ref=pick(ref, target),
            send_sem=halo_send.at[direction, part],
            recv_sem=halo_recv.at[direction, part],
            device_id=(to, half),
            device_id_type=MESH,
        )

    up = [halo(0, 2, depth + 2, lax.rem(slab + slabs - 1, slabs), part) for part in range(2)]
    down = [halo(1, depth, 0, lax.rem(slab + 1, slabs), part) for part in range(2)]

    @pl.when(first)
    def _():
        raw[:, 0:2] = jnp.zeros((3, 2, members, width), jnp.float32)
        mushy[0:2] = jnp.zeros((2, 8, width), jnp.float32)

    @pl.when(last)
    def _():
        raw[:, depth + 2 : depth + 4] = jnp.zeros((3, 2, members, width), jnp.float32)
        mushy[depth + 2 : depth + 4] = jnp.zeros((2, 8, width), jnp.float32)

    pl.semaphore_wait(barrier, everyone - 1)

    @pl.when(jnp.logical_not(first))
    def _():
        for copy in up:
            copy.start()

    @pl.when(jnp.logical_not(last))
    def _():
        for copy in down:
            copy.start()

    pieces = []

    def send(field, start, count):
        number = len(pieces)
        copies = []
        for hop in range(1, halves):
            copies.append(
                pltpu.make_async_remote_copy(
                    src_ref=own.at[field, pl.ds(start, count)],
                    dst_ref=other.at[hop - 1, field, pl.ds(start, count)],
                    send_sem=state_send.at[hop - 1, number],
                    recv_sem=state_recv.at[hop - 1, number],
                    device_id=(slab, lax.rem(half + hop, halves)),
                    device_id_type=MESH,
                )
            )
        for copy in copies:
            copy.start()
        pieces.append((field, start, count, copies))

    middle = depth // 2
    send(SPEED, 2, middle - 2)
    send(SPEED, middle, middle - 2)
    relayout_pair(range(2, depth - 2))

    def inner_pair(group, carry):
        at = pl.ds(pl.multiple_of(group * 8, 8), 8)
        mask = mushy[2 : depth + 2]
        before = raw[SPEED, 2 : depth + 2, at, :]
        heat, solute = advance_pair(
            raw[HEAT, 2 : depth + 2, at, :], raw[SOLUTE, 2 : depth + 2, at, :], before, mask
        )
        heat, solute = advance_pair(heat, solute, advance_speed(before, mask), mask[1:-1])
        own[HEAT, 2 : depth - 2, at, :] = heat
        own[SOLUTE, 2 : depth - 2, at, :] = solute
        return carry

    lax.fori_loop(0, groups, inner_pair, 0)

    @pl.when(jnp.logical_not(last))
    def _():
        for copy in up:
            copy.wait_recv()

    @pl.when(jnp.logical_not(first))
    def _():
        for copy in down:
            copy.wait_recv()

    def edges(group, carry):
        at = pl.ds(pl.multiple_of(group * 8, 8), 8)
        for begin, outside, edge in ((0, first, 0), (depth - 2, last, 3)):
            mask = mushy[begin : begin + 6]
            before = raw[SPEED, begin : begin + 6, at, :]
            heat, solute = advance_pair(
                raw[HEAT, begin : begin + 6, at, :], raw[SOLUTE, begin : begin + 6, at, :], before, mask
            )
            speed = advance_speed(before, mask)
            row = lax.broadcasted_iota(jnp.int32, heat.shape, 0)
            beyond = jnp.logical_and(row == edge, outside)
            heat, solute, speed = [jnp.where(beyond, 0.0, q) for q in (heat, solute, speed)]
            mask = mask[1:-1]
            new_heat, new_solute = advance_pair(heat, solute, speed, mask)
            own[HEAT, begin : begin + 2, at, :] = new_heat
            own[SOLUTE, begin : begin + 2, at, :] = new_solute
            own[SPEED, begin : begin + 2, at, :] = advance_speed(speed, mask)
        return carry

    lax.fori_loop(0, groups, edges, 0)

    lane = lax.broadcasted_iota(jnp.int32, (members, width), 1)
    per_slab = index_ref.shape[0]
    for load in load_observed:
        load.wait()
    observed = jnp.zeros((members, width), jnp.float32)
    value = jnp.zeros((members, width), jnp.float32)
    error = jnp.ones((members, width), jnp.float32)
    for o in range(per_slab):
        cell = index_ref[o]
        z = cell // width
        w = cell - z * width
        factor = 1.0 - mushy[z + 2][0:1] * (1.0 - mushy_ratio)
        temp = jnp.where(lane == w, own[HEAT, z] * factor, 0.0)
        observed = jnp.where(lane == o, jnp.sum(temp, axis=1, keepdims=True), observed)
        value = jnp.where(lane == o, value_ref[o], value)
        error = jnp.where(lane == o, error_ref[o], error)
    square[...] = jnp.zeros((ens, width), jnp.float32)
    square[pl.ds(pl.multiple_of(half * members, 8), members), :] = (observed - value) / error
    turned = square[...].T
    seen[me] = turned[0:8] + pltpu.roll(turned[8:16], ens // 2, 1)

    def tell_copy(peer):
        return pltpu.make_async_remote_copy(
            src_ref=seen.at[me],
            dst_ref=seen.at[me],
            send_sem=seen_send.at[0],
            recv_sem=seen_recv.at[0],
            device_id=(peer // halves, lax.rem(peer, halves)),
            device_id_type=MESH,
        )

    def tell(step, carry):
        tell_copy(lax.rem(me + step, everyone)).start()
        return carry

    lax.fori_loop(1, everyone, tell, 0)

    for field in (SPEED, HEAT, SOLUTE):
        send(field, 0, 2)
        send(field, depth - 2, 2)
        if field != SPEED:
            send(field, 2, middle - 2)
            send(field, middle, middle - 2)

    rest = seen.at[pl.ds(0, everyone - 1)]
    pltpu.make_async_copy(rest, rest, seen_recv.at[0]).wait()

    got = seen[...].reshape(slabs, halves, 8, ens)
    place = lax.broadcasted_iota(jnp.int32, (slabs, 8, ens), 2)
    low = jnp.zeros((slabs, 8, ens), jnp.float32)
    high = jnp.zeros((slabs, 8, ens), jnp.float32)
    for m in range(halves):
        mine = (place >= m * members) & (place < (m + 1) * members)
        low = jnp.where(mine, got[:, m], low)
        high = jnp.where(mine, pltpu.roll(got[:, m], ens // 2, 2), high)
    deviation = jnp.concatenate(
        [low.reshape(slabs * 8, ens), high.reshape(slabs * 8, ens)], axis=0
    )
    mean = jnp.sum(deviation, axis=1, keepdims=True) * (1.0 / ens)
    root = 1.0 / (ens - 1.0) ** 0.5
    spread = (deviation - mean) * root
    project = -jnp.sum(spread * mean, axis=0, keepdims=True)
    gram = lax.dot_general(
        spread, spread, (((0,), (0,)), ((), ())),
        precision=HIGHEST, preferred_element_type=jnp.float32,
    )
    rows = lax.broadcasted_iota(jnp.int32, (ens, ens), 0)
    lanes = lax.broadcasted_iota(jnp.int32, (ens, ens), 1)
    square[...] = jnp.where(rows == lanes, 1.0, 0.0) + gram
    inverse_factor(square)
    inverse = square[...]
    shift = jnp.sum(inverse * project, axis=1, keepdims=True)
    shift = jnp.sum(inverse * shift, axis=0, keepdims=True)
    combined = inverse + shift * root
    combined = combined - jnp.sum(combined, axis=1, keepdims=True) * (1.0 / ens) + 1.0 / ens
    square[...] = pltpu.roll(combined, lax.rem(ens - half * members, ens), 1)
    weight_high, weight_low = split(square[pl.ds(pl.multiple_of(half * members, 8), members), :])
    weights = jnp.concatenate([weight_high, weight_high, weight_low], axis=1)

    for field, start, count, copies in pieces:
        for copy in copies:
            copy.wait_recv()
        for z in range(start, start + count, 2):
            parts = []
            for d in (z, z + 1):
                blocks = [own[field, d]] + [
                    other[halves - q - 1, field, d] for q in range(1, halves)
                ]
                parts.append(jnp.concatenate(blocks, axis=0))
            state_high, state_low = split(jnp.concatenate(parts, axis=1))
            mixed = jnp.dot(
                weights,
                jnp.concatenate([state_high, state_low, state_high], axis=0),
                preferred_element_type=jnp.float32,
            )
            for i, d in enumerate((z, z + 1)):
                block = mixed[:, i * width : (i + 1) * width]
                if field == SPEED:
                    out_v_ref[pl.ds(d, members, stride=depth), :] = block
                else:
                    out_hc_ref[pl.ds(field * depth + d, members, stride=2 * depth), :] = block

    for _, _, _, copies in pieces:
        for copy in copies:
            copy.wait_send()
    pltpu.make_async_copy(rest, rest, seen_send.at[0]).wait()

    @pl.when(jnp.logical_not(first))
    def _():
        for copy in up:
            copy.wait_send()

    @pl.when(jnp.logical_not(last))
    def _():
        for copy in down:
            copy.wait_send()


def on_device(slabs, halves, member_heat_solute, velocity, phase_mask, obs_index, obs_value, obs_error):
    members, _, depth, width = member_heat_solute.shape
    ens = members * halves
    held = pl.BlockSpec(memory_space=pltpu.VMEM)
    anywhere = pl.BlockSpec(memory_space=pltpu.HBM)
    hc, vel = pl.pallas_call(
        functools.partial(kernel, slabs, halves),
        out_shape=(
            pltpu.VMEM((members * 2 * depth, width), jnp.float32),
            pltpu.VMEM((members * depth, width), jnp.float32),
        ),
        in_specs=[anywhere] * 6,
        out_specs=(held, held),
        scratch_shapes=[
            pltpu.VMEM((depth, width), jnp.int32),
            pltpu.SMEM(obs_index.shape, jnp.int32),
            pltpu.SMEM(obs_value.shape, jnp.float32),
            pltpu.SMEM(obs_error.shape, jnp.float32),
            pltpu.VMEM((members * 2 * depth, width), jnp.float32),
            pltpu.VMEM((members * depth, width), jnp.float32),
            pltpu.VMEM((3, depth + 4, members, width), jnp.float32),
            pltpu.VMEM((depth + 4, 8, width), jnp.float32),
            pltpu.VMEM((3, depth, members, width), jnp.float32),
            pltpu.VMEM((halves - 1, 3, depth, members, width), jnp.float32),
            pltpu.VMEM((slabs * halves, 8, ens), jnp.float32),
            pltpu.VMEM((ens, ens), jnp.float32),
            pltpu.SemaphoreType.DMA((6,)),
            pltpu.SemaphoreType.DMA((2, 2)),
            pltpu.SemaphoreType.DMA((2, 2)),
            pltpu.SemaphoreType.DMA((halves - 1, 12)),
            pltpu.SemaphoreType.DMA((halves - 1, 12)),
            pltpu.SemaphoreType.DMA((1,)),
            pltpu.SemaphoreType.DMA((1,)),
        ],
        compiler_params=pltpu.CompilerParams(
            collective_id=0, has_side_effects=True, vmem_limit_bytes=40 * 1024 * 1024
        ),
    )(
        *[
            pltpu.with_memory_space_constraint(x, pltpu.HBM)
            for x in (
                member_heat_solute.reshape(-1, width),
                velocity.reshape(-1, width),
                phase_mask,
                obs_index,
                obs_value,
                obs_error,
            )
        ]
    )
    return hc.reshape(members, 2, depth, width), vel.reshape(members, depth, width)


def solution(mesh):
    return jax.shard_map(
        functools.partial(on_device, mesh.shape["space"], mesh.shape["mem"]),
        mesh=mesh,
        in_specs=(
            P("mem", None, "space", None),
            P("mem", "space", None),
            P("space", None),
            P("space"),
            P("space"),
            P("space"),
        ),
        out_specs=(P("mem", None, "space", None), P("mem", "space", None)),
        check_vma=False,
    )
```

```python
import functools

import jax
import jax.numpy as jnp
from jax import lax
from jax.experimental import pallas as pl
from jax.experimental.pallas import tpu as pltpu
from jax.sharding import PartitionSpec as P

heat_diffusion = 0.15
advection = 0.4
solute_diffusion = 0.05
segregation = 0.3
momentum_diffusion = 0.1
darcy_drag = 0.5
mushy_ratio = 1.0 / 3.0

MESH = pl.DeviceIdType.MESH
HIGHEST = lax.Precision.HIGHEST
HEAT, SOLUTE, SPEED = 0, 1, 2
PANEL = 16


def lateral_sum(field):
    lane = lax.broadcasted_iota(jnp.int32, field.shape, 2)
    last = field.shape[2] - 1
    left = jnp.where(lane == 0, field, pltpu.roll(field, 1, 2))
    right = jnp.where(lane == last, field, pltpu.roll(field, last, 2))
    return left + right


def laplacian(field):
    centre = field[1:-1]
    return field[2:] + field[:-2] + lateral_sum(centre) - 4.0 * centre


def advance_speed(speed, mushy):
    centre = speed[1:-1]
    return centre + momentum_diffusion * laplacian(speed) - darcy_drag * mushy[1:-1] * centre


def advance_pair(heat, solute, speed, mushy):
    temp = heat * (1.0 - mushy * (1.0 - mushy_ratio))
    drift = advection * speed[1:-1]
    new_heat = (
        heat[1:-1] + heat_diffusion * laplacian(temp) - drift * (heat[1:-1] - heat[:-2])
    )
    new_solute = (
        solute[1:-1]
        + solute_diffusion * laplacian(solute)
        - drift * (solute[1:-1] - solute[:-2])
        + segregation * mushy[1:-1] * (temp[1:-1] - solute[1:-1])
    )
    return new_heat, new_solute


def split(values):
    high = values.astype(jnp.bfloat16)
    low = (values - high.astype(jnp.float32)).astype(jnp.bfloat16)
    return high, low


def split_three(values):
    parts = []
    for _ in range(3):
        part = values.astype(jnp.bfloat16).astype(jnp.float32)
        parts.append(part)
        values = values - part
    return parts


def inverse_factor(matrix_ref):
    order = matrix_ref.shape[0]
    lane = lax.broadcasted_iota(jnp.int32, (PANEL, order), 1)
    sub = lax.broadcasted_iota(jnp.int32, (PANEL, order), 0)
    rows = lax.broadcasted_iota(jnp.int32, (order, order), 0)
    lanes = lax.broadcasted_iota(jnp.int32, (order, order), 1)

    def panel(block, carry):
        base = pl.multiple_of(block * PANEL, PANEL)
        here = matrix_ref[pl.ds(base, PANEL), :]
        cols = [
            jnp.broadcast_to(
                jnp.sum(jnp.where(lane == base + s, here, 0.0), axis=1, keepdims=True),
                (PANEL, order),
            )
            for s in range(PANEL)
        ]
        upper = jnp.where(lane >= base, here, 0.0)
        inverse = jnp.where(lane < base, here, jnp.where(lane == base + sub, 1.0, 0.0))
        diagonal = jnp.zeros((PANEL, order), jnp.float32)
        for s in range(PANEL):
            pivot = cols[s][s : s + 1]
            diagonal = jnp.where(sub == s, pivot, diagonal)
            factor = jnp.where(sub > s, cols[s] / pivot, 0.0)
            upper = upper - factor * upper[s : s + 1]
            inverse = inverse - factor * inverse[s : s + 1]
            for t in range(s + 1, PANEL):
                cols[t] = cols[t] - factor * cols[t][s : s + 1]
        scale = 1.0 / jnp.sqrt(diagonal)
        upper = upper * scale
        inverse = inverse * scale
        right = jnp.where(lane < base + PANEL, inverse, upper)
        upper_parts = split_three(upper)
        right_parts = split_three(right)
        change = lax.dot_general(
            jnp.concatenate([upper_parts[i] for i in (0, 0, 1, 1, 0, 2)], axis=0).astype(jnp.bfloat16),
            jnp.concatenate([right_parts[i] for i in (0, 1, 0, 1, 2, 0)], axis=0).astype(jnp.bfloat16),
            (((0,), (0,)), ((), ())),
            preferred_element_type=jnp.float32,
        )
        old = matrix_ref[...]
        kept = jnp.where((lanes >= base) & (lanes < base + PANEL), 0.0, old)
        matrix_ref[...] = jnp.where(rows >= base + PANEL, kept - change, old)
        matrix_ref[pl.ds(base, PANEL), :] = inverse
        return carry

    lax.fori_loop(0, order // PANEL, panel, 0)


def kernel(
    slabs, halves,
    hc_ref, v_ref, phase_ref, cell_ref, datum_ref, deviate_ref,
    out_hc_ref, out_v_ref,
    mask_ref, index_ref, value_ref, error_ref, hc, vel, raw, mushy, own, other, seen, square,
    in_sem, halo_send, halo_recv, state_send, state_recv, seen_send, seen_recv,
):
    members = own.shape[2]
    width = own.shape[3]
    depth = own.shape[1]
    groups = members // 8
    everyone = slabs * halves
    ens = members * halves
    slab = lax.axis_index("space")
    half = lax.axis_index("mem")
    me = slab * halves + half
    first = slab == 0
    last = slab == slabs - 1

    load_v = pltpu.make_async_copy(v_ref, vel, in_sem.at[0])
    load_hc = pltpu.make_async_copy(hc_ref, hc, in_sem.at[1])
    load_mask = pltpu.make_async_copy(phase_ref, mask_ref, in_sem.at[2])
    load_observed = [
        pltpu.make_async_copy(cell_ref, index_ref, in_sem.at[3]),
        pltpu.make_async_copy(datum_ref, value_ref, in_sem.at[4]),
        pltpu.make_async_copy(deviate_ref, error_ref, in_sem.at[5]),
    ]
    load_mask.start()
    load_v.start()
    load_hc.start()
    for load in load_observed:
        load.start()

    barrier = pltpu.get_barrier_semaphore()

    def greet(step, carry):
        peer = lax.rem(me + step, everyone)
        pl.semaphore_signal(
            barrier, inc=1, device_id=(peer // halves, lax.rem(peer, halves)), device_id_type=MESH
        )
        return carry

    lax.fori_loop(1, everyone, greet, 0)

    load_mask.wait()
    for z in range(depth):
        row = mask_ref[z : z + 1, :].astype(jnp.float32)
        mushy[z + 2] = jnp.broadcast_to(row, (8, width))

    def relayout_speed(zs):
        for z in zs:
            raw[SPEED, z + 2] = vel[pl.ds(z, members, stride=depth), :]

    def relayout_pair(zs):
        for z in zs:
            raw[HEAT, z + 2] = hc[pl.ds(z, members, stride=2 * depth), :]
            raw[SOLUTE, z + 2] = hc[pl.ds(depth + z, members, stride=2 * depth), :]

    load_v.wait()
    relayout_speed(range(depth))

    def inner_speed(group, carry):
        at = pl.ds(pl.multiple_of(group * 8, 8), 8)
        mask = mushy[2 : depth + 2]
        speed = advance_speed(raw[SPEED, 2 : depth + 2, at, :], mask)
        own[SPEED, 2 : depth - 2, at, :] = advance_speed(speed, mask[1:-1])
        return carry

    lax.fori_loop(0, groups, inner_speed, 0)
    load_hc.wait()
    relayout_pair((0, 1, depth - 2, depth - 1))

    def halo(direction, source, target, to, part):
        ref = raw if part == 0 else mushy
        pick = (lambda r, a: r.at[:, pl.ds(a, 2)]) if part == 0 else (lambda r, a: r.at[pl.ds(a, 2)])
        return pltpu.make_async_remote_copy(
            src_ref=pick(ref, source),
            dst_ref=pick(ref, target),
            send_sem=halo_send.at[direction, part],
            recv_sem=halo_recv.at[direction, part],
            device_id=(to, half),
            device_id_type=MESH,
        )

    up = [halo(0, 2, depth + 2, lax.rem(slab + slabs - 1, slabs), part) for part in range(2)]
    down = [halo(1, depth, 0, lax.rem(slab + 1, slabs), part) for part in range(2)]

    @pl.when(first)
    def _():
        raw[:, 0:2] = jnp.zeros((3, 2, members, width), jnp.float32)
        mushy[0:2] = jnp.zeros((2, 8, width), jnp.float32)

    @pl.when(last)
    def _():
        raw[:, depth + 2 : depth + 4] = jnp.zeros((3, 2, members, width), jnp.float32)
        mushy[depth + 2 : depth + 4] = jnp.zeros((2, 8, width), jnp.float32)

    pl.semaphore_wait(barrier, everyone - 1)

    @pl.when(jnp.logical_not(first))
    def _():
        for copy in up:
            copy.start()

    @pl.when(jnp.logical_not(last))
    def _():
        for copy in down:
            copy.start()

    pieces = []

    def send(field, start, count):
        number = len(pieces)
        copies = []
        for hop in range(1, halves):
            copies.append(
                pltpu.make_async_remote_copy(
                    src_ref=own.at[field, pl.ds(start, count)],
                    dst_ref=other.at[hop - 1, field, pl.ds(start, count)],
                    send_sem=state_send.at[hop - 1, number],
                    recv_sem=state_recv.at[hop - 1, number],
                    device_id=(slab, lax.rem(half + hop, halves)),
                    device_id_type=MESH,
                )
            )
        for copy in copies:
            copy.start()
        pieces.append((field, start, count, copies))

    middle = depth // 2
    for z in range(2, depth - 2, 2):
        send(SPEED, z, 2)
    relayout_pair(range(2, depth - 2))

    def inner_pair(group, carry):
        at = pl.ds(pl.multiple_of(group * 8, 8), 8)
        mask = mushy[2 : depth + 2]
        before = raw[SPEED, 2 : depth + 2, at, :]
        heat, solute = advance_pair(
            raw[HEAT, 2 : depth + 2, at, :], raw[SOLUTE, 2 : depth + 2, at, :], before, mask
        )
        heat, solute = advance_pair(heat, solute, advance_speed(before, mask), mask[1:-1])
        own[HEAT, 2 : depth - 2, at, :] = heat
        own[SOLUTE, 2 : depth - 2, at, :] = solute
        return carry

    lax.fori_loop(0, groups, inner_pair, 0)
    for z in range(2, middle, 2):
        send(HEAT, z, 2)

    @pl.when(jnp.logical_not(last))
    def _():
        for copy in up:
            copy.wait_recv()

    @pl.when(jnp.logical_not(first))
    def _():
        for copy in down:
            copy.wait_recv()

    def edges(group, carry):
        at = pl.ds(pl.multiple_of(group * 8, 8), 8)
        for begin, outside, edge in ((0, first, 0), (depth - 2, last, 3)):
            mask = mushy[begin : begin + 6]
            before = raw[SPEED, begin : begin + 6, at, :]
            heat, solute = advance_pair(
                raw[HEAT, begin : begin + 6, at, :], raw[SOLUTE, begin : begin + 6, at, :], before, mask
            )
            speed = advance_speed(before, mask)
            row = lax.broadcasted_iota(jnp.int32, heat.shape, 0)
            beyond = jnp.logical_and(row == edge, outside)
            heat, solute, speed = [jnp.where(beyond, 0.0, q) for q in (heat, solute, speed)]
            mask = mask[1:-1]
            new_heat, new_solute = advance_pair(heat, solute, speed, mask)
            own[HEAT, begin : begin + 2, at, :] = new_heat
            own[SOLUTE, begin : begin + 2, at, :] = new_solute
            own[SPEED, begin : begin + 2, at, :] = advance_speed(speed, mask)
        return carry

    lax.fori_loop(0, groups, edges, 0)

    lane = lax.broadcasted_iota(jnp.int32, (members, width), 1)
    per_slab = index_ref.shape[0]
    for load in load_observed:
        load.wait()
    observed = jnp.zeros((members, width), jnp.float32)
    value = jnp.zeros((members, width), jnp.float32)
    error = jnp.ones((members, width), jnp.float32)
    for o in range(per_slab):
        cell = index_ref[o]
        z = cell // width
        w = cell - z * width
        factor = 1.0 - mushy[z + 2][0:1] * (1.0 - mushy_ratio)
        temp = jnp.where(lane == w, own[HEAT, z] * factor, 0.0)
        observed = jnp.where(lane == o, jnp.sum(temp, axis=1, keepdims=True), observed)
        value = jnp.where(lane == o, value_ref[o], value)
        error = jnp.where(lane == o, error_ref[o], error)
    square[...] = jnp.zeros((ens, width), jnp.float32)
    square[pl.ds(pl.multiple_of(half * members, 8), members), :] = (observed - value) / error
    turned = square[...].T
    seen[me] = turned[0:8] + pltpu.roll(turned[8:16], ens // 2, 1)

    def tell_copy(peer):
        return pltpu.make_async_remote_copy(
            src_ref=seen.at[me],
            dst_ref=seen.at[me],
            send_sem=seen_send.at[0],
            recv_sem=seen_recv.at[0],
            device_id=(peer // halves, lax.rem(peer, halves)),
            device_id_type=MESH,
        )

    def tell(step, carry):
        tell_copy(lax.rem(me + step, everyone)).start()
        return carry

    lax.fori_loop(1, everyone, tell, 0)

    for z in (0, depth - 2):
        send(SPEED, z, 2)
    for z in (0, *range(middle, depth, 2)):
        send(HEAT, z, 2)
    for z in range(0, depth, 2):
        send(SOLUTE, z, 2)

    rest = seen.at[pl.ds(0, everyone - 1)]
    pltpu.make_async_copy(rest, rest, seen_recv.at[0]).wait()

    got = seen[...].reshape(slabs, halves, 8, ens)
    place = lax.broadcasted_iota(jnp.int32, (slabs, 8, ens), 2)
    low = jnp.zeros((slabs, 8, ens), jnp.float32)
    high = jnp.zeros((slabs, 8, ens), jnp.float32)
    for m in range(halves):
        mine = (place >= m * members) & (place < (m + 1) * members)
        low = jnp.where(mine, got[:, m], low)
        high = jnp.where(mine, pltpu.roll(got[:, m], ens // 2, 2), high)
    deviation = jnp.concatenate(
        [low.reshape(slabs * 8, ens), high.reshape(slabs * 8, ens)], axis=0
    )
    mean = jnp.sum(deviation, axis=1, keepdims=True) * (1.0 / ens)
    root = 1.0 / (ens - 1.0) ** 0.5
    spread = (deviation - mean) * root
    project = -jnp.sum(spread * mean, axis=0, keepdims=True)
    gram = lax.dot_general(
        spread, spread, (((0,), (0,)), ((), ())),
        precision=HIGHEST, preferred_element_type=jnp.float32,
    )
    rows = lax.broadcasted_iota(jnp.int32, (ens, ens), 0)
    lanes = lax.broadcasted_iota(jnp.int32, (ens, ens), 1)
    square[...] = jnp.where(rows == lanes, 1.0, 0.0) + gram
    inverse_factor(square)
    inverse = square[...]
    shift = jnp.sum(inverse * project, axis=1, keepdims=True)
    shift = jnp.sum(inverse * shift, axis=0, keepdims=True)
    combined = inverse + shift * root
    combined = combined - jnp.sum(combined, axis=1, keepdims=True) * (1.0 / ens) + 1.0 / ens
    square[...] = pltpu.roll(combined, lax.rem(ens - half * members, ens), 1)
    weight_high, weight_low = split(square[pl.ds(pl.multiple_of(half * members, 8), members), :])
    weights = jnp.concatenate([weight_high, weight_high, weight_low], axis=1)

    for field, start, count, copies in pieces:
        for copy in copies:
            copy.wait_recv()
        for z in range(start, start + count, 2):
            parts = []
            for d in (z, z + 1):
                blocks = [own[field, d]] + [
                    other[halves - q - 1, field, d] for q in range(1, halves)
                ]
                parts.append(jnp.concatenate(blocks, axis=0))
            state_high, state_low = split(jnp.concatenate(parts, axis=1))
            mixed = jnp.dot(
                weights,
                jnp.concatenate([state_high, state_low, state_high], axis=0),
                preferred_element_type=jnp.float32,
            )
            for i, d in enumerate((z, z + 1)):
                block = mixed[:, i * width : (i + 1) * width]
                if field == SPEED:
                    out_v_ref[pl.ds(d, members, stride=depth), :] = block
                else:
                    out_hc_ref[pl.ds(field * depth + d, members, stride=2 * depth), :] = block

    for _, _, _, copies in pieces:
        for copy in copies:
            copy.wait_send()
    pltpu.make_async_copy(rest, rest, seen_send.at[0]).wait()

    @pl.when(jnp.logical_not(first))
    def _():
        for copy in up:
            copy.wait_send()

    @pl.when(jnp.logical_not(last))
    def _():
        for copy in down:
            copy.wait_send()


def on_device(slabs, halves, member_heat_solute, velocity, phase_mask, obs_index, obs_value, obs_error):
    members, _, depth, width = member_heat_solute.shape
    ens = members * halves
    held = pl.BlockSpec(memory_space=pltpu.VMEM)
    anywhere = pl.BlockSpec(memory_space=pltpu.HBM)
    hc, vel = pl.pallas_call(
        functools.partial(kernel, slabs, halves),
        out_shape=(
            pltpu.VMEM((members * 2 * depth, width), jnp.float32),
            pltpu.VMEM((members * depth, width), jnp.float32),
        ),
        in_specs=[anywhere] * 6,
        out_specs=(held, held),
        scratch_shapes=[
            pltpu.VMEM((depth, width), jnp.int32),
            pltpu.SMEM(obs_index.shape, jnp.int32),
            pltpu.SMEM(obs_value.shape, jnp.float32),
            pltpu.SMEM(obs_error.shape, jnp.float32),
            pltpu.VMEM((members * 2 * depth, width), jnp.float32),
            pltpu.VMEM((members * depth, width), jnp.float32),
            pltpu.VMEM((3, depth + 4, members, width), jnp.float32),
            pltpu.VMEM((depth + 4, 8, width), jnp.float32),
            pltpu.VMEM((3, depth, members, width), jnp.float32),
            pltpu.VMEM((halves - 1, 3, depth, members, width), jnp.float32),
            pltpu.VMEM((slabs * halves, 8, ens), jnp.float32),
            pltpu.VMEM((ens, ens), jnp.float32),
            pltpu.SemaphoreType.DMA((6,)),
            pltpu.SemaphoreType.DMA((2, 2)),
            pltpu.SemaphoreType.DMA((2, 2)),
            pltpu.SemaphoreType.DMA((halves - 1, 3 * depth // 2)),
            pltpu.SemaphoreType.DMA((halves - 1, 3 * depth // 2)),
            pltpu.SemaphoreType.DMA((1,)),
            pltpu.SemaphoreType.DMA((1,)),
        ],
        compiler_params=pltpu.CompilerParams(
            collective_id=0, has_side_effects=True, vmem_limit_bytes=40 * 1024 * 1024
        ),
    )(
        *[
            pltpu.with_memory_space_constraint(x, pltpu.HBM)
            for x in (
                member_heat_solute.reshape(-1, width),
                velocity.reshape(-1, width),
                phase_mask,
                obs_index,
                obs_value,
                obs_error,
            )
        ]
    )
    return hc.reshape(members, 2, depth, width), vel.reshape(members, depth, width)


def solution(mesh):
    return jax.shard_map(
        functools.partial(on_device, mesh.shape["space"], mesh.shape["mem"]),
        mesh=mesh,
        in_specs=(
            P("mem", None, "space", None),
            P("mem", "space", None),
            P("space", None),
            P("space"),
            P("space"),
            P("space"),
        ),
        out_specs=(P("mem", None, "space", None), P("mem", "space", None)),
        check_vma=False,
    )
```

```python
import functools

import jax
import jax.numpy as jnp
from jax import lax
from jax.experimental import pallas as pl
from jax.experimental.pallas import tpu as pltpu
from jax.sharding import PartitionSpec as P

heat_diffusion = 0.15
advection = 0.4
solute_diffusion = 0.05
segregation = 0.3
momentum_diffusion = 0.1
darcy_drag = 0.5
mushy_ratio = 1.0 / 3.0

MESH = pl.DeviceIdType.MESH
HIGHEST = lax.Precision.HIGHEST
HEAT, SOLUTE, SPEED = 0, 1, 2
PANEL = 16


def lateral_sum(field):
    lane = lax.broadcasted_iota(jnp.int32, field.shape, 2)
    last = field.shape[2] - 1
    left = jnp.where(lane == 0, field, pltpu.roll(field, 1, 2))
    right = jnp.where(lane == last, field, pltpu.roll(field, last, 2))
    return left + right


def laplacian(field):
    centre = field[1:-1]
    return field[2:] + field[:-2] + lateral_sum(centre) - 4.0 * centre


def advance_speed(speed, mushy):
    centre = speed[1:-1]
    return centre + momentum_diffusion * laplacian(speed) - darcy_drag * mushy[1:-1] * centre


def advance_pair(heat, solute, speed, mushy):
    temp = heat * (1.0 - mushy * (1.0 - mushy_ratio))
    drift = advection * speed[1:-1]
    new_heat = (
        heat[1:-1] + heat_diffusion * laplacian(temp) - drift * (heat[1:-1] - heat[:-2])
    )
    new_solute = (
        solute[1:-1]
        + solute_diffusion * laplacian(solute)
        - drift * (solute[1:-1] - solute[:-2])
        + segregation * mushy[1:-1] * (temp[1:-1] - solute[1:-1])
    )
    return new_heat, new_solute


def split(values):
    high = values.astype(jnp.bfloat16)
    low = (values - high.astype(jnp.float32)).astype(jnp.bfloat16)
    return high, low


def split_three(values):
    parts = []
    for _ in range(3):
        part = values.astype(jnp.bfloat16).astype(jnp.float32)
        parts.append(part)
        values = values - part
    return parts


def inverse_factor(matrix_ref):
    order = matrix_ref.shape[0]
    lane = lax.broadcasted_iota(jnp.int32, (PANEL, order), 1)
    sub = lax.broadcasted_iota(jnp.int32, (PANEL, order), 0)
    rows = lax.broadcasted_iota(jnp.int32, (order, order), 0)
    lanes = lax.broadcasted_iota(jnp.int32, (order, order), 1)

    def panel(block, carry):
        base = pl.multiple_of(block * PANEL, PANEL)
        here = matrix_ref[pl.ds(base, PANEL), :]
        cols = [
            jnp.broadcast_to(
                jnp.sum(jnp.where(lane == base + s, here, 0.0), axis=1, keepdims=True),
                (PANEL, order),
            )
            for s in range(PANEL)
        ]
        upper = jnp.where(lane >= base, here, 0.0)
        inverse = jnp.where(lane < base, here, jnp.where(lane == base + sub, 1.0, 0.0))
        diagonal = jnp.zeros((PANEL, order), jnp.float32)
        for s in range(PANEL):
            pivot = cols[s][s : s + 1]
            diagonal = jnp.where(sub == s, pivot, diagonal)
            factor = jnp.where(sub > s, cols[s] / pivot, 0.0)
            upper = upper - factor * upper[s : s + 1]
            inverse = inverse - factor * inverse[s : s + 1]
            for t in range(s + 1, PANEL):
                cols[t] = cols[t] - factor * cols[t][s : s + 1]
        scale = 1.0 / jnp.sqrt(diagonal)
        upper = upper * scale
        inverse = inverse * scale
        right = jnp.where(lane < base + PANEL, inverse, upper)
        upper_parts = split_three(upper)
        right_parts = split_three(right)
        change = lax.dot_general(
            jnp.concatenate([upper_parts[i] for i in (0, 0, 1, 1, 0, 2)], axis=0).astype(jnp.bfloat16),
            jnp.concatenate([right_parts[i] for i in (0, 1, 0, 1, 2, 0)], axis=0).astype(jnp.bfloat16),
            (((0,), (0,)), ((), ())),
            preferred_element_type=jnp.float32,
        )
        old = matrix_ref[...]
        kept = jnp.where((lanes >= base) & (lanes < base + PANEL), 0.0, old)
        matrix_ref[...] = jnp.where(rows >= base + PANEL, kept - change, old)
        matrix_ref[pl.ds(base, PANEL), :] = inverse
        return carry

    lax.fori_loop(0, order // PANEL, panel, 0)


def kernel(
    slabs, halves,
    hc_ref, v_ref, phase_ref, cell_ref, datum_ref, deviate_ref,
    out_hc_ref, out_v_ref,
    mask_ref, index_ref, value_ref, error_ref, hc, vel, raw, mushy, own, other, sums, seen, square,
    in_sem, halo_send, halo_recv, state_send, state_recv, seen_send, seen_recv, sum_send, sum_recv,
):
    members = own.shape[2]
    width = own.shape[3]
    depth = own.shape[1]
    groups = members // 8
    everyone = slabs * halves
    ens = members * halves
    slab = lax.axis_index("space")
    half = lax.axis_index("mem")
    me = slab * halves + half
    first = slab == 0
    last = slab == slabs - 1

    load_v = pltpu.make_async_copy(v_ref, vel, in_sem.at[0])
    load_hc = pltpu.make_async_copy(hc_ref, hc, in_sem.at[1])
    load_mask = pltpu.make_async_copy(phase_ref, mask_ref, in_sem.at[2])
    load_observed = [
        pltpu.make_async_copy(cell_ref, index_ref, in_sem.at[3]),
        pltpu.make_async_copy(datum_ref, value_ref, in_sem.at[4]),
        pltpu.make_async_copy(deviate_ref, error_ref, in_sem.at[5]),
    ]
    load_mask.start()
    load_v.start()
    load_hc.start()
    for load in load_observed:
        load.start()

    barrier = pltpu.get_barrier_semaphore()

    def greet(step, carry):
        peer = lax.rem(me + step, everyone)
        pl.semaphore_signal(
            barrier, inc=1, device_id=(peer // halves, lax.rem(peer, halves)), device_id_type=MESH
        )
        return carry

    lax.fori_loop(1, everyone, greet, 0)

    load_mask.wait()
    for z in range(depth):
        row = mask_ref[z : z + 1, :].astype(jnp.float32)
        mushy[z + 2] = jnp.broadcast_to(row, (8, width))

    def relayout_speed(zs):
        for z in zs:
            raw[SPEED, z + 2] = vel[pl.ds(z, members, stride=depth), :]

    def relayout_pair(zs):
        for z in zs:
            raw[HEAT, z + 2] = hc[pl.ds(z, members, stride=2 * depth), :]
            raw[SOLUTE, z + 2] = hc[pl.ds(depth + z, members, stride=2 * depth), :]

    load_v.wait()
    relayout_speed(range(depth))

    def inner_speed(group, carry):
        at = pl.ds(pl.multiple_of(group * 8, 8), 8)
        mask = mushy[2 : depth + 2]
        speed = advance_speed(raw[SPEED, 2 : depth + 2, at, :], mask)
        own[SPEED, 2 : depth - 2, at, :] = advance_speed(speed, mask[1:-1])
        return carry

    lax.fori_loop(0, groups, inner_speed, 0)
    load_hc.wait()
    relayout_pair((0, 1, depth - 2, depth - 1))

    def halo(direction, source, target, to, part):
        ref = raw if part == 0 else mushy
        pick = (lambda r, a: r.at[:, pl.ds(a, 2)]) if part == 0 else (lambda r, a: r.at[pl.ds(a, 2)])
        return pltpu.make_async_remote_copy(
            src_ref=pick(ref, source),
            dst_ref=pick(ref, target),
            send_sem=halo_send.at[direction, part],
            recv_sem=halo_recv.at[direction, part],
            device_id=(to, half),
            device_id_type=MESH,
        )

    up = [halo(0, 2, depth + 2, lax.rem(slab + slabs - 1, slabs), part) for part in range(2)]
    down = [halo(1, depth, 0, lax.rem(slab + 1, slabs), part) for part in range(2)]

    @pl.when(first)
    def _():
        raw[:, 0:2] = jnp.zeros((3, 2, members, width), jnp.float32)
        mushy[0:2] = jnp.zeros((2, 8, width), jnp.float32)

    @pl.when(last)
    def _():
        raw[:, depth + 2 : depth + 4] = jnp.zeros((3, 2, members, width), jnp.float32)
        mushy[depth + 2 : depth + 4] = jnp.zeros((2, 8, width), jnp.float32)

    pl.semaphore_wait(barrier, everyone - 1)

    @pl.when(jnp.logical_not(first))
    def _():
        for copy in up:
            copy.start()

    @pl.when(jnp.logical_not(last))
    def _():
        for copy in down:
            copy.start()

    pieces = []

    def send(field, start, count):
        number = len(pieces)
        copies = []
        for hop in range(1, halves):
            copies.append(
                pltpu.make_async_remote_copy(
                    src_ref=own.at[field, pl.ds(start, count)],
                    dst_ref=other.at[hop - 1, field, pl.ds(start, count)],
                    send_sem=state_send.at[hop - 1, number],
                    recv_sem=state_recv.at[hop - 1, number],
                    device_id=(slab, lax.rem(half + hop, halves)),
                    device_id_type=MESH,
                )
            )
        for hop, copy in enumerate(copies, 1):
            pl.when(half + hop < halves)(copy.start)
        pieces.append((field, start, count, copies))

    middle = depth // 2
    for z in range(2, depth - 2, 2):
        send(SPEED, z, 2)
    relayout_pair(range(2, depth - 2))

    def inner_pair(group, carry):
        at = pl.ds(pl.multiple_of(group * 8, 8), 8)
        mask = mushy[2 : depth + 2]
        before = raw[SPEED, 2 : depth + 2, at, :]
        heat, solute = advance_pair(
            raw[HEAT, 2 : depth + 2, at, :], raw[SOLUTE, 2 : depth + 2, at, :], before, mask
        )
        heat, solute = advance_pair(heat, solute, advance_speed(before, mask), mask[1:-1])
        own[HEAT, 2 : depth - 2, at, :] = heat
        own[SOLUTE, 2 : depth - 2, at, :] = solute
        return carry

    lax.fori_loop(0, groups, inner_pair, 0)
    for z in range(2, middle, 2):
        send(HEAT, z, 2)

    @pl.when(jnp.logical_not(last))
    def _():
        for copy in up:
            copy.wait_recv()

    @pl.when(jnp.logical_not(first))
    def _():
        for copy in down:
            copy.wait_recv()

    def edges(group, carry):
        at = pl.ds(pl.multiple_of(group * 8, 8), 8)
        for begin, outside, edge in ((0, first, 0), (depth - 2, last, 3)):
            mask = mushy[begin : begin + 6]
            before = raw[SPEED, begin : begin + 6, at, :]
            heat, solute = advance_pair(
                raw[HEAT, begin : begin + 6, at, :], raw[SOLUTE, begin : begin + 6, at, :], before, mask
            )
            speed = advance_speed(before, mask)
            row = lax.broadcasted_iota(jnp.int32, heat.shape, 0)
            beyond = jnp.logical_and(row == edge, outside)
            heat, solute, speed = [jnp.where(beyond, 0.0, q) for q in (heat, solute, speed)]
            mask = mask[1:-1]
            new_heat, new_solute = advance_pair(heat, solute, speed, mask)
            own[HEAT, begin : begin + 2, at, :] = new_heat
            own[SOLUTE, begin : begin + 2, at, :] = new_solute
            own[SPEED, begin : begin + 2, at, :] = advance_speed(speed, mask)
        return carry

    lax.fori_loop(0, groups, edges, 0)

    lane = lax.broadcasted_iota(jnp.int32, (members, width), 1)
    per_slab = index_ref.shape[0]
    for load in load_observed:
        load.wait()
    observed = jnp.zeros((members, width), jnp.float32)
    value = jnp.zeros((members, width), jnp.float32)
    error = jnp.ones((members, width), jnp.float32)
    for o in range(per_slab):
        cell = index_ref[o]
        z = cell // width
        w = cell - z * width
        factor = 1.0 - mushy[z + 2][0:1] * (1.0 - mushy_ratio)
        temp = jnp.where(lane == w, own[HEAT, z] * factor, 0.0)
        observed = jnp.where(lane == o, jnp.sum(temp, axis=1, keepdims=True), observed)
        value = jnp.where(lane == o, value_ref[o], value)
        error = jnp.where(lane == o, error_ref[o], error)
    square[...] = jnp.zeros((ens, width), jnp.float32)
    square[pl.ds(pl.multiple_of(half * members, 8), members), :] = (observed - value) / error
    turned = square[...].T
    seen[me] = turned[0:8] + pltpu.roll(turned[8:16], ens // 2, 1)

    def tell_copy(peer):
        return pltpu.make_async_remote_copy(
            src_ref=seen.at[me],
            dst_ref=seen.at[me],
            send_sem=seen_send.at[0],
            recv_sem=seen_recv.at[0],
            device_id=(peer // halves, lax.rem(peer, halves)),
            device_id_type=MESH,
        )

    def tell(step, carry):
        tell_copy(lax.rem(me + step, everyone)).start()
        return carry

    lax.fori_loop(1, everyone, tell, 0)

    for z in (0, depth - 2):
        send(SPEED, z, 2)
    for z in (0, *range(middle, depth, 2)):
        send(HEAT, z, 2)
    for z in range(0, depth, 2):
        send(SOLUTE, z, 2)

    for hop in range(1, halves):

        @pl.when(half < hop)
        def _():
            other[hop - 1, :, :, 8:, :] = jnp.zeros((3, depth, members - 8, width), jnp.float32)

    rest = seen.at[pl.ds(0, everyone - 1)]
    pltpu.make_async_copy(rest, rest, seen_recv.at[0]).wait()

    got = seen[...].reshape(slabs, halves, 8, ens)
    place = lax.broadcasted_iota(jnp.int32, (slabs, 8, ens), 2)
    low = jnp.zeros((slabs, 8, ens), jnp.float32)
    high = jnp.zeros((slabs, 8, ens), jnp.float32)
    for m in range(halves):
        mine = (place >= m * members) & (place < (m + 1) * members)
        low = jnp.where(mine, got[:, m], low)
        high = jnp.where(mine, pltpu.roll(got[:, m], ens // 2, 2), high)
    deviation = jnp.concatenate(
        [low.reshape(slabs * 8, ens), high.reshape(slabs * 8, ens)], axis=0
    )
    mean = jnp.sum(deviation, axis=1, keepdims=True) * (1.0 / ens)
    root = 1.0 / (ens - 1.0) ** 0.5
    spread = (deviation - mean) * root
    project = -jnp.sum(spread * mean, axis=0, keepdims=True)
    gram = lax.dot_general(
        spread, spread, (((0,), (0,)), ((), ())),
        precision=HIGHEST, preferred_element_type=jnp.float32,
    )
    rows = lax.broadcasted_iota(jnp.int32, (ens, ens), 0)
    lanes = lax.broadcasted_iota(jnp.int32, (ens, ens), 1)
    square[...] = jnp.where(rows == lanes, 1.0, 0.0) + gram
    inverse_factor(square)
    inverse = square[...]
    shift = jnp.sum(inverse * project, axis=1, keepdims=True)
    shift = jnp.sum(inverse * shift, axis=0, keepdims=True)
    combined = inverse + shift * root
    level = (1.0 - jnp.sum(combined, axis=1, keepdims=True)) * (1.0 / ens)
    combined = combined + level
    shift_column = jnp.sum(jnp.where(rows == lanes, shift, 0.0), axis=1, keepdims=True) * root
    square[...] = jnp.broadcast_to(shift_column, (ens, width))
    own_rows = pl.ds(pl.multiple_of(half * members, 8), members)

    @pl.when(half > 0)
    def _():
        own_shift = square[own_rows, :]
        sub = lax.broadcasted_iota(jnp.int32, (8, width), 0)

        def add_up(z, carry):
            for field in range(3):
                state = own[field, z]
                plain = jnp.sum(state, axis=0, keepdims=True)
                shifted = jnp.sum(state * own_shift, axis=0, keepdims=True)
                sums[field, z] = jnp.where(sub == 0, plain, jnp.where(sub == 1, shifted, 0.0))
            return carry

        lax.fori_loop(0, depth, add_up, 0)

    sum_copies = [
        pltpu.make_async_remote_copy(
            src_ref=sums,
            dst_ref=other.at[hop - 1, :, :, pl.ds(0, 8), :],
            send_sem=sum_send.at[hop - 1],
            recv_sem=sum_recv.at[hop - 1],
            device_id=(slab, lax.rem(half + hop, halves)),
            device_id_type=MESH,
        )
        for hop in range(1, halves)
    ]
    for hop, copy in enumerate(sum_copies, 1):
        pl.when(half + hop >= halves)(copy.start)

    combined = pltpu.roll(combined, lax.rem(ens - half * members, ens), 1)
    ahead = lanes // members
    at = lanes - ahead * members
    of_sums = jnp.where(at == 0, level, jnp.where(at == 1, 1.0, 0.0))
    square[...] = jnp.where((ahead > 0) & (half + ahead < halves), of_sums, combined)
    for hop, copy in enumerate(sum_copies, 1):
        pl.when(half < hop)(copy.wait_recv)
    weight_high, weight_low = split(square[own_rows, :])
    weights = jnp.concatenate([weight_high, weight_high, weight_low], axis=1)

    for field, start, count, copies in pieces:
        for hop, copy in enumerate(copies, 1):
            pl.when(half >= hop)(copy.wait_recv)
        for z in range(start, start + count, 2):
            parts = []
            for d in (z, z + 1):
                blocks = [own[field, d]] + [
                    other[halves - q - 1, field, d] for q in range(1, halves)
                ]
                parts.append(jnp.concatenate(blocks, axis=0))
            state_high, state_low = split(jnp.concatenate(parts, axis=1))
            mixed = jnp.dot(
                weights,
                jnp.concatenate([state_high, state_low, state_high], axis=0),
                preferred_element_type=jnp.float32,
            )
            for i, d in enumerate((z, z + 1)):
                block = mixed[:, i * width : (i + 1) * width]
                if field == SPEED:
                    out_v_ref[pl.ds(d, members, stride=depth), :] = block
                else:
                    out_hc_ref[pl.ds(field * depth + d, members, stride=2 * depth), :] = block

    for _, _, _, copies in pieces:
        for hop, copy in enumerate(copies, 1):
            pl.when(half + hop < halves)(copy.wait_send)
    for hop, copy in enumerate(sum_copies, 1):
        pl.when(half + hop >= halves)(copy.wait_send)
    pltpu.make_async_copy(rest, rest, seen_send.at[0]).wait()

    @pl.when(jnp.logical_not(first))
    def _():
        for copy in up:
            copy.wait_send()

    @pl.when(jnp.logical_not(last))
    def _():
        for copy in down:
            copy.wait_send()


def on_device(slabs, halves, member_heat_solute, velocity, phase_mask, obs_index, obs_value, obs_error):
    members, _, depth, width = member_heat_solute.shape
    ens = members * halves
    held = pl.BlockSpec(memory_space=pltpu.VMEM)
    anywhere = pl.BlockSpec(memory_space=pltpu.HBM)
    hc, vel = pl.pallas_call(
        functools.partial(kernel, slabs, halves),
        out_shape=(
            pltpu.VMEM((members * 2 * depth, width), jnp.float32),
            pltpu.VMEM((members * depth, width), jnp.float32),
        ),
        in_specs=[anywhere] * 6,
        out_specs=(held, held),
        scratch_shapes=[
            pltpu.VMEM((depth, width), jnp.int32),
            pltpu.SMEM(obs_index.shape, jnp.int32),
            pltpu.SMEM(obs_value.shape, jnp.float32),
            pltpu.SMEM(obs_error.shape, jnp.float32),
            pltpu.VMEM((members * 2 * depth, width), jnp.float32),
            pltpu.VMEM((members * depth, width), jnp.float32),
            pltpu.VMEM((3, depth + 4, members, width), jnp.float32),
            pltpu.VMEM((depth + 4, 8, width), jnp.float32),
            pltpu.VMEM((3, depth, members, width), jnp.float32),
            pltpu.VMEM((halves - 1, 3, depth, members, width), jnp.float32),
            pltpu.VMEM((3, depth, 8, width), jnp.float32),
            pltpu.VMEM((slabs * halves, 8, ens), jnp.float32),
            pltpu.VMEM((ens, ens), jnp.float32),
            pltpu.SemaphoreType.DMA((6,)),
            pltpu.SemaphoreType.DMA((2, 2)),
            pltpu.SemaphoreType.DMA((2, 2)),
            pltpu.SemaphoreType.DMA((halves - 1, 3 * depth // 2)),
            pltpu.SemaphoreType.DMA((halves - 1, 3 * depth // 2)),
            pltpu.SemaphoreType.DMA((1,)),
            pltpu.SemaphoreType.DMA((1,)),
            pltpu.SemaphoreType.DMA((halves - 1,)),
            pltpu.SemaphoreType.DMA((halves - 1,)),
        ],
        compiler_params=pltpu.CompilerParams(
            collective_id=0, has_side_effects=True, vmem_limit_bytes=40 * 1024 * 1024
        ),
    )(
        *[
            pltpu.with_memory_space_constraint(x, pltpu.HBM)
            for x in (
                member_heat_solute.reshape(-1, width),
                velocity.reshape(-1, width),
                phase_mask,
                obs_index,
                obs_value,
                obs_error,
            )
        ]
    )
    return hc.reshape(members, 2, depth, width), vel.reshape(members, depth, width)


def solution(mesh):
    return jax.shard_map(
        functools.partial(on_device, mesh.shape["space"], mesh.shape["mem"]),
        mesh=mesh,
        in_specs=(
            P("mem", None, "space", None),
            P("mem", "space", None),
            P("space", None),
            P("space"),
            P("space"),
            P("space"),
        ),
        out_specs=(P("mem", None, "space", None), P("mem", "space", None)),
        check_vma=False,
    )
```

```python
import functools

import jax
import jax.numpy as jnp
from jax import lax
from jax.experimental import pallas as pl
from jax.experimental.pallas import tpu as pltpu
from jax.sharding import PartitionSpec as P

heat_diffusion = 0.15
advection = 0.4
solute_diffusion = 0.05
segregation = 0.3
momentum_diffusion = 0.1
darcy_drag = 0.5
mushy_ratio = 1.0 / 3.0

MESH = pl.DeviceIdType.MESH
HIGHEST = lax.Precision.HIGHEST
HEAT, SOLUTE, SPEED = 0, 1, 2
PANEL = 16


def lateral_sum(field):
    lane = lax.broadcasted_iota(jnp.int32, field.shape, 2)
    last = field.shape[2] - 1
    left = jnp.where(lane == 0, field, pltpu.roll(field, 1, 2))
    right = jnp.where(lane == last, field, pltpu.roll(field, last, 2))
    return left + right


def laplacian(field):
    centre = field[1:-1]
    return field[2:] + field[:-2] + lateral_sum(centre) - 4.0 * centre


def advance_speed(speed, mushy):
    centre = speed[1:-1]
    return centre + momentum_diffusion * laplacian(speed) - darcy_drag * mushy[1:-1] * centre


def advance_pair(heat, solute, speed, mushy):
    temp = heat * (1.0 - mushy * (1.0 - mushy_ratio))
    drift = advection * speed[1:-1]
    new_heat = (
        heat[1:-1] + heat_diffusion * laplacian(temp) - drift * (heat[1:-1] - heat[:-2])
    )
    new_solute = (
        solute[1:-1]
        + solute_diffusion * laplacian(solute)
        - drift * (solute[1:-1] - solute[:-2])
        + segregation * mushy[1:-1] * (temp[1:-1] - solute[1:-1])
    )
    return new_heat, new_solute


def split(values):
    high = values.astype(jnp.bfloat16)
    low = (values - high.astype(jnp.float32)).astype(jnp.bfloat16)
    return high, low


def split_three(values):
    parts = []
    for _ in range(3):
        part = values.astype(jnp.bfloat16).astype(jnp.float32)
        parts.append(part)
        values = values - part
    return parts


def inverse_factor(matrix_ref):
    order = matrix_ref.shape[0]
    lane = lax.broadcasted_iota(jnp.int32, (PANEL, order), 1)
    sub = lax.broadcasted_iota(jnp.int32, (PANEL, order), 0)
    rows = lax.broadcasted_iota(jnp.int32, (order, order), 0)
    lanes = lax.broadcasted_iota(jnp.int32, (order, order), 1)

    def panel(block, carry):
        base = pl.multiple_of(block * PANEL, PANEL)
        here = matrix_ref[pl.ds(base, PANEL), :]
        cols = [
            jnp.broadcast_to(
                jnp.sum(jnp.where(lane == base + s, here, 0.0), axis=1, keepdims=True),
                (PANEL, order),
            )
            for s in range(PANEL)
        ]
        upper = jnp.where(lane >= base, here, 0.0)
        inverse = jnp.where(lane < base, here, jnp.where(lane == base + sub, 1.0, 0.0))
        diagonal = jnp.zeros((PANEL, order), jnp.float32)
        for s in range(PANEL):
            pivot = cols[s][s : s + 1]
            diagonal = jnp.where(sub == s, pivot, diagonal)
            factor = jnp.where(sub > s, cols[s] / pivot, 0.0)
            upper = upper - factor * upper[s : s + 1]
            inverse = inverse - factor * inverse[s : s + 1]
            for t in range(s + 1, PANEL):
                cols[t] = cols[t] - factor * cols[t][s : s + 1]
        scale = 1.0 / jnp.sqrt(diagonal)
        upper = upper * scale
        inverse = inverse * scale
        right = jnp.where(lane < base + PANEL, inverse, upper)
        upper_parts = split_three(upper)
        right_parts = split_three(right)
        change = lax.dot_general(
            jnp.concatenate([upper_parts[i] for i in (0, 0, 1, 1, 0, 2)], axis=0).astype(jnp.bfloat16),
            jnp.concatenate([right_parts[i] for i in (0, 1, 0, 1, 2, 0)], axis=0).astype(jnp.bfloat16),
            (((0,), (0,)), ((), ())),
            preferred_element_type=jnp.float32,
        )
        old = matrix_ref[...]
        kept = jnp.where((lanes >= base) & (lanes < base + PANEL), 0.0, old)
        matrix_ref[...] = jnp.where(rows >= base + PANEL, kept - change, old)
        matrix_ref[pl.ds(base, PANEL), :] = inverse
        return carry

    lax.fori_loop(0, order // PANEL, panel, 0)


def kernel(
    slabs, halves,
    hc_ref, v_ref, phase_ref, cell_ref, datum_ref, deviate_ref,
    out_hc_ref, out_v_ref,
    mask_ref, index_ref, value_ref, error_ref, hc, vel, raw, mushy, own, other, sums, sums_in, part, seen, square,
    in_sem, halo_send, halo_recv, state_send, state_recv, part_send, part_recv, seen_send, seen_recv, sum_send, sum_recv,
):
    members = own.shape[2]
    width = own.shape[3]
    depth = own.shape[1]
    groups = members // 8
    ens = members * halves
    slab = lax.axis_index("space")
    half = lax.axis_index("mem")
    first = slab == 0
    last = slab == slabs - 1

    load_v = pltpu.make_async_copy(v_ref, vel, in_sem.at[0])
    load_hc = pltpu.make_async_copy(hc_ref, hc, in_sem.at[1])
    load_mask = pltpu.make_async_copy(phase_ref, mask_ref, in_sem.at[2])
    load_observed = [
        pltpu.make_async_copy(cell_ref, index_ref, in_sem.at[3]),
        pltpu.make_async_copy(datum_ref, value_ref, in_sem.at[4]),
        pltpu.make_async_copy(deviate_ref, error_ref, in_sem.at[5]),
    ]
    load_mask.start()
    load_v.start()
    load_hc.start()
    for load in load_observed:
        load.start()

    barrier = pltpu.get_barrier_semaphore()

    def greet(step, carry):
        pl.semaphore_signal(
            barrier, inc=1, device_id=(lax.rem(slab + step, slabs), half), device_id_type=MESH
        )
        return carry

    for hop in range(1, halves):
        pl.semaphore_signal(
            barrier, inc=1, device_id=(slab, lax.rem(half + hop, halves)), device_id_type=MESH
        )
    lax.fori_loop(1, slabs, greet, 0)

    load_mask.wait()
    for z in range(depth):
        row = mask_ref[z : z + 1, :].astype(jnp.float32)
        mushy[z + 2] = jnp.broadcast_to(row, (8, width))

    def relayout_speed(zs):
        for z in zs:
            raw[SPEED, z + 2] = vel[pl.ds(z, members, stride=depth), :]

    def relayout_pair(zs):
        for z in zs:
            raw[HEAT, z + 2] = hc[pl.ds(z, members, stride=2 * depth), :]
            raw[SOLUTE, z + 2] = hc[pl.ds(depth + z, members, stride=2 * depth), :]

    load_v.wait()
    relayout_speed(range(depth))

    def inner_speed(group, carry):
        at = pl.ds(pl.multiple_of(group * 8, 8), 8)
        mask = mushy[2 : depth + 2]
        speed = advance_speed(raw[SPEED, 2 : depth + 2, at, :], mask)
        own[SPEED, 2 : depth - 2, at, :] = advance_speed(speed, mask[1:-1])
        return carry

    lax.fori_loop(0, groups, inner_speed, 0)
    load_hc.wait()
    relayout_pair((0, 1, depth - 2, depth - 1))

    def halo(direction, source, target, to, part):
        ref = raw if part == 0 else mushy
        pick = (lambda r, a: r.at[:, pl.ds(a, 2)]) if part == 0 else (lambda r, a: r.at[pl.ds(a, 2)])
        return pltpu.make_async_remote_copy(
            src_ref=pick(ref, source),
            dst_ref=pick(ref, target),
            send_sem=halo_send.at[direction, part],
            recv_sem=halo_recv.at[direction, part],
            device_id=(to, half),
            device_id_type=MESH,
        )

    up = [halo(0, 2, depth + 2, lax.rem(slab + slabs - 1, slabs), part) for part in range(2)]
    down = [halo(1, depth, 0, lax.rem(slab + 1, slabs), part) for part in range(2)]

    @pl.when(first)
    def _():
        raw[:, 0:2] = jnp.zeros((3, 2, members, width), jnp.float32)
        mushy[0:2] = jnp.zeros((2, 8, width), jnp.float32)

    @pl.when(last)
    def _():
        raw[:, depth + 2 : depth + 4] = jnp.zeros((3, 2, members, width), jnp.float32)
        mushy[depth + 2 : depth + 4] = jnp.zeros((2, 8, width), jnp.float32)

    pl.semaphore_wait(barrier, slabs + halves - 2)

    @pl.when(jnp.logical_not(first))
    def _():
        for copy in up:
            copy.start()

    @pl.when(jnp.logical_not(last))
    def _():
        for copy in down:
            copy.start()

    pieces = []

    def send(field, start, count):
        number = len(pieces)
        copies = []
        for hop in range(1, halves):
            copies.append(
                pltpu.make_async_remote_copy(
                    src_ref=own.at[field, pl.ds(start, count)],
                    dst_ref=other.at[hop - 1, field, pl.ds(start, count)],
                    send_sem=state_send.at[hop - 1, number],
                    recv_sem=state_recv.at[hop - 1, number],
                    device_id=(slab, lax.rem(half + hop, halves)),
                    device_id_type=MESH,
                )
            )
        for hop, copy in enumerate(copies, 1):
            pl.when(half + hop < halves)(copy.start)
        pieces.append((field, start, count, copies))

    middle = depth // 2
    for z in range(2, depth - 2, 2):
        send(SPEED, z, 2)
    relayout_pair(range(2, depth - 2))

    def inner_pair(group, carry):
        at = pl.ds(pl.multiple_of(group * 8, 8), 8)
        mask = mushy[2 : depth + 2]
        before = raw[SPEED, 2 : depth + 2, at, :]
        heat, solute = advance_pair(
            raw[HEAT, 2 : depth + 2, at, :], raw[SOLUTE, 2 : depth + 2, at, :], before, mask
        )
        heat, solute = advance_pair(heat, solute, advance_speed(before, mask), mask[1:-1])
        own[HEAT, 2 : depth - 2, at, :] = heat
        own[SOLUTE, 2 : depth - 2, at, :] = solute
        return carry

    lax.fori_loop(0, groups, inner_pair, 0)
    for z in range(2, middle, 2):
        send(HEAT, z, 2)

    @pl.when(jnp.logical_not(last))
    def _():
        for copy in up:
            copy.wait_recv()

    @pl.when(jnp.logical_not(first))
    def _():
        for copy in down:
            copy.wait_recv()

    def edges(group, carry):
        at = pl.ds(pl.multiple_of(group * 8, 8), 8)
        for begin, outside, edge in ((0, first, 0), (depth - 2, last, 3)):
            mask = mushy[begin : begin + 6]
            before = raw[SPEED, begin : begin + 6, at, :]
            heat, solute = advance_pair(
                raw[HEAT, begin : begin + 6, at, :], raw[SOLUTE, begin : begin + 6, at, :], before, mask
            )
            speed = advance_speed(before, mask)
            row = lax.broadcasted_iota(jnp.int32, heat.shape, 0)
            beyond = jnp.logical_and(row == edge, outside)
            heat, solute, speed = [jnp.where(beyond, 0.0, q) for q in (heat, solute, speed)]
            mask = mask[1:-1]
            new_heat, new_solute = advance_pair(heat, solute, speed, mask)
            own[HEAT, begin : begin + 2, at, :] = new_heat
            own[SOLUTE, begin : begin + 2, at, :] = new_solute
            own[SPEED, begin : begin + 2, at, :] = advance_speed(speed, mask)
        return carry

    lax.fori_loop(0, groups, edges, 0)

    lane = lax.broadcasted_iota(jnp.int32, (members, width), 1)
    per_slab = index_ref.shape[0]
    for load in load_observed:
        load.wait()
    observed = jnp.zeros((members, width), jnp.float32)
    value = jnp.zeros((members, width), jnp.float32)
    error = jnp.ones((members, width), jnp.float32)
    for o in range(per_slab):
        cell = index_ref[o]
        z = cell // width
        w = cell - z * width
        factor = 1.0 - mushy[z + 2][0:1] * (1.0 - mushy_ratio)
        temp = jnp.where(lane == w, own[HEAT, z] * factor, 0.0)
        observed = jnp.where(lane == o, jnp.sum(temp, axis=1, keepdims=True), observed)
        value = jnp.where(lane == o, value_ref[o], value)
        error = jnp.where(lane == o, error_ref[o], error)
    square[...] = jnp.zeros((ens, width), jnp.float32)
    square[pl.ds(pl.multiple_of(half * members, 8), members), :] = (observed - value) / error
    turned = square[...].T
    part[half] = turned[0:8] + pltpu.roll(turned[8:16], ens // 2, 1)
    part_copies = [
        pltpu.make_async_remote_copy(
            src_ref=part.at[half],
            dst_ref=part.at[half],
            send_sem=part_send.at[hop - 1],
            recv_sem=part_recv.at[0],
            device_id=(slab, lax.rem(half + hop, halves)),
            device_id_type=MESH,
        )
        for hop in range(1, halves)
    ]
    for copy in part_copies:
        copy.start()

    for z in (0, depth - 2):
        send(SPEED, z, 2)
    for z in (0, *range(middle, depth, 2)):
        send(HEAT, z, 2)
    for z in range(0, depth, 2):
        send(SOLUTE, z, 2)

    for hop in range(1, halves):

        @pl.when(half < hop)
        def _():
            other[hop - 1, :, :, 8:, :] = jnp.zeros((3, depth, members - 8, width), jnp.float32)

    others = part.at[pl.ds(0, halves - 1)]
    pltpu.make_async_copy(others, others, part_recv.at[0]).wait()
    place = lax.broadcasted_iota(jnp.int32, (8, ens), 1)
    low = jnp.zeros((8, ens), jnp.float32)
    high = jnp.zeros((8, ens), jnp.float32)
    for m in range(halves):
        mine = (place >= m * members) & (place < (m + 1) * members)
        low = jnp.where(mine, part[m], low)
        high = jnp.where(mine, pltpu.roll(part[m], ens // 2, 1), high)
    seen[slab, 0:8] = low
    seen[slab, 8:16] = high

    def tell(step, carry):
        pltpu.make_async_remote_copy(
            src_ref=seen.at[slab],
            dst_ref=seen.at[slab],
            send_sem=seen_send.at[0],
            recv_sem=seen_recv.at[0],
            device_id=(lax.rem(slab + step, slabs), half),
            device_id_type=MESH,
        ).start()
        return carry

    lax.fori_loop(1, slabs, tell, 0)

    for hop in range(1, halves):

        @pl.when(half < hop)
        def _():
            other[hop - 1, :, :, 8:, :] = jnp.zeros((3, depth, members - 8, width), jnp.float32)

    rest = seen.at[pl.ds(0, slabs - 1)]
    pltpu.make_async_copy(rest, rest, seen_recv.at[0]).wait()

    deviation = seen[...].reshape(slabs * 16, ens)
    mean = jnp.sum(deviation, axis=1, keepdims=True) * (1.0 / ens)
    root = 1.0 / (ens - 1.0) ** 0.5
    spread = (deviation - mean) * root
    project = -jnp.sum(spread * mean, axis=0, keepdims=True)
    gram = lax.dot_general(
        spread, spread, (((0,), (0,)), ((), ())),
        precision=HIGHEST, preferred_element_type=jnp.float32,
    )
    rows = lax.broadcasted_iota(jnp.int32, (ens, ens), 0)
    lanes = lax.broadcasted_iota(jnp.int32, (ens, ens), 1)
    square[...] = jnp.where(rows == lanes, 1.0, 0.0) + gram
    inverse_factor(square)
    inverse = square[...]
    shift = jnp.sum(inverse * project, axis=1, keepdims=True)
    shift = jnp.sum(inverse * shift, axis=0, keepdims=True)
    combined = inverse + shift * root
    level = (1.0 - jnp.sum(combined, axis=1, keepdims=True)) * (1.0 / ens)
    combined = combined + level
    shift_column = jnp.sum(jnp.where(rows == lanes, shift, 0.0), axis=1, keepdims=True) * root
    square[...] = jnp.broadcast_to(shift_column, (ens, width))
    own_rows = pl.ds(pl.multiple_of(half * members, 8), members)

    @pl.when(half > 0)
    def _():
        own_shift = square[own_rows, :]
        for z in range(depth):
            for field in range(3):
                state = own[field, z]
                sums[field, 0, z : z + 1, :] = jnp.sum(state, axis=0, keepdims=True)
                sums[field, 1, z : z + 1, :] = jnp.sum(state * own_shift, axis=0, keepdims=True)

    sum_copies = [
        pltpu.make_async_remote_copy(
            src_ref=sums,
            dst_ref=sums_in.at[hop - 1],
            send_sem=sum_send.at[hop - 1],
            recv_sem=sum_recv.at[hop - 1],
            device_id=(slab, lax.rem(half + hop, halves)),
            device_id_type=MESH,
        )
        for hop in range(1, halves)
    ]
    for hop, copy in enumerate(sum_copies, 1):
        pl.when(half + hop >= halves)(copy.start)

    combined = pltpu.roll(combined, lax.rem(ens - half * members, ens), 1)
    ahead = lanes // members
    at = lanes - ahead * members
    of_sums = jnp.where(at == 0, level, jnp.where(at == 1, 1.0, 0.0))
    square[...] = jnp.where((ahead > 0) & (half + ahead < halves), of_sums, combined)
    for hop, copy in enumerate(sum_copies, 1):

        @pl.when(half < hop)
        def _():
            copy.wait_recv()
            sub = lax.broadcasted_iota(jnp.int32, (8, width), 0)
            for field in range(3):
                for z in range(depth):
                    plain = sums_in[hop - 1, field, 0, z : z + 1, :]
                    shifted = sums_in[hop - 1, field, 1, z : z + 1, :]
                    other[hop - 1, field, z, 0:8, :] = jnp.where(
                        sub == 0, plain, jnp.where(sub == 1, shifted, 0.0)
                    )

    weight_high, weight_low = split(square[own_rows, :])
    weights = jnp.concatenate([weight_high, weight_high, weight_low], axis=1)

    for field, start, count, copies in pieces:
        for hop, copy in enumerate(copies, 1):
            pl.when(half >= hop)(copy.wait_recv)
        for z in range(start, start + count, 2):
            parts = []
            for d in (z, z + 1):
                blocks = [own[field, d]] + [
                    other[halves - q - 1, field, d] for q in range(1, halves)
                ]
                parts.append(jnp.concatenate(blocks, axis=0))
            state_high, state_low = split(jnp.concatenate(parts, axis=1))
            mixed = jnp.dot(
                weights,
                jnp.concatenate([state_high, state_low, state_high], axis=0),
                preferred_element_type=jnp.float32,
            )
            for i, d in enumerate((z, z + 1)):
                block = mixed[:, i * width : (i + 1) * width]
                if field == SPEED:
                    out_v_ref[pl.ds(d, members, stride=depth), :] = block
                else:
                    out_hc_ref[pl.ds(field * depth + d, members, stride=2 * depth), :] = block

    for _, _, _, copies in pieces:
        for hop, copy in enumerate(copies, 1):
            pl.when(half + hop < halves)(copy.wait_send)
    for hop, copy in enumerate(sum_copies, 1):
        pl.when(half + hop >= halves)(copy.wait_send)
    for copy in part_copies:
        copy.wait_send()
    pltpu.make_async_copy(rest, rest, seen_send.at[0]).wait()

    @pl.when(jnp.logical_not(first))
    def _():
        for copy in up:
            copy.wait_send()

    @pl.when(jnp.logical_not(last))
    def _():
        for copy in down:
            copy.wait_send()


def write_back(hc, vel, out_hc, out_vel, sem):
    copies = [
        pltpu.make_async_copy(hc, out_hc, sem.at[0]),
        pltpu.make_async_copy(vel, out_vel, sem.at[1]),
    ]
    for copy in copies:
        copy.start()
    for copy in copies:
        copy.wait()


def on_device(slabs, halves, member_heat_solute, velocity, phase_mask, obs_index, obs_value, obs_error):
    members, _, depth, width = member_heat_solute.shape
    ens = members * halves
    held = pl.BlockSpec(memory_space=pltpu.VMEM)
    anywhere = pl.BlockSpec(memory_space=pltpu.HBM)
    hc, vel = pl.pallas_call(
        functools.partial(kernel, slabs, halves),
        out_shape=(
            pltpu.VMEM((members * 2 * depth, width), jnp.float32),
            pltpu.VMEM((members * depth, width), jnp.float32),
        ),
        in_specs=[anywhere] * 6,
        out_specs=(held, held),
        scratch_shapes=[
            pltpu.VMEM((depth, width), jnp.int32),
            pltpu.SMEM(obs_index.shape, jnp.int32),
            pltpu.SMEM(obs_value.shape, jnp.float32),
            pltpu.SMEM(obs_error.shape, jnp.float32),
            pltpu.VMEM((members * 2 * depth, width), jnp.float32),
            pltpu.VMEM((members * depth, width), jnp.float32),
            pltpu.VMEM((3, depth + 4, members, width), jnp.float32),
            pltpu.VMEM((depth + 4, 8, width), jnp.float32),
            pltpu.VMEM((3, depth, members, width), jnp.float32),
            pltpu.VMEM((halves - 1, 3, depth, members, width), jnp.float32),
            pltpu.VMEM((3, 2, depth, width), jnp.float32),
            pltpu.VMEM((halves - 1, 3, 2, depth, width), jnp.float32),
            pltpu.VMEM((halves, 8, ens), jnp.float32),
            pltpu.VMEM((slabs, 16, ens), jnp.float32),
            pltpu.VMEM((ens, ens), jnp.float32),
            pltpu.SemaphoreType.DMA((6,)),
            pltpu.SemaphoreType.DMA((2, 2)),
            pltpu.SemaphoreType.DMA((2, 2)),
            pltpu.SemaphoreType.DMA((halves - 1, 3 * depth // 2)),
            pltpu.SemaphoreType.DMA((halves - 1, 3 * depth // 2)),
            pltpu.SemaphoreType.DMA((halves - 1,)),
            pltpu.SemaphoreType.DMA((1,)),
            pltpu.SemaphoreType.DMA((1,)),
            pltpu.SemaphoreType.DMA((1,)),
            pltpu.SemaphoreType.DMA((halves - 1,)),
            pltpu.SemaphoreType.DMA((halves - 1,)),
        ],
        compiler_params=pltpu.CompilerParams(
            collective_id=0, has_side_effects=True, vmem_limit_bytes=40 * 1024 * 1024
        ),
    )(
        *[
            pltpu.with_memory_space_constraint(x, pltpu.HBM)
            for x in (
                member_heat_solute.reshape(-1, width),
                velocity.reshape(-1, width),
                phase_mask,
                obs_index,
                obs_value,
                obs_error,
            )
        ]
    )
    hc, vel = pl.pallas_call(
        write_back,
        out_shape=(
            jax.ShapeDtypeStruct(hc.shape, jnp.float32),
            jax.ShapeDtypeStruct(vel.shape, jnp.float32),
        ),
        in_specs=[held, held],
        out_specs=(anywhere, anywhere),
        scratch_shapes=[pltpu.SemaphoreType.DMA((2,))],
        compiler_params=pltpu.CompilerParams(vmem_limit_bytes=16 * 1024 * 1024),
    )(
        pltpu.with_memory_space_constraint(hc, pltpu.VMEM),
        pltpu.with_memory_space_constraint(vel, pltpu.VMEM),
    )
    return hc.reshape(members, 2, depth, width), vel.reshape(members, depth, width)


def solution(mesh):
    return jax.shard_map(
        functools.partial(on_device, mesh.shape["space"], mesh.shape["mem"]),
        mesh=mesh,
        in_specs=(
            P("mem", None, "space", None),
            P("mem", "space", None),
            P("space", None),
            P("space"),
            P("space"),
            P("space"),
        ),
        out_specs=(P("mem", None, "space", None), P("mem", "space", None)),
        check_vma=False,
    )
```

```python
import functools

import jax
import jax.numpy as jnp
from jax import lax
from jax.experimental import pallas as pl
from jax.experimental.pallas import tpu as pltpu
from jax.sharding import PartitionSpec as P

heat_diffusion = 0.15
advection = 0.4
solute_diffusion = 0.05
segregation = 0.3
momentum_diffusion = 0.1
darcy_drag = 0.5
mushy_ratio = 1.0 / 3.0

MESH = pl.DeviceIdType.MESH
HIGHEST = lax.Precision.HIGHEST
HEAT, SOLUTE, SPEED = 0, 1, 2
PANEL = 16


def lateral_sum(field):
    lane = lax.broadcasted_iota(jnp.int32, field.shape, 2)
    last = field.shape[2] - 1
    left = jnp.where(lane == 0, field, pltpu.roll(field, 1, 2))
    right = jnp.where(lane == last, field, pltpu.roll(field, last, 2))
    return left + right


def laplacian(field):
    centre = field[1:-1]
    return field[2:] + field[:-2] + lateral_sum(centre) - 4.0 * centre


def advance_speed(speed, mushy):
    centre = speed[1:-1]
    return centre + momentum_diffusion * laplacian(speed) - darcy_drag * mushy[1:-1] * centre


def advance_pair(heat, solute, speed, mushy):
    temp = heat * (1.0 - mushy * (1.0 - mushy_ratio))
    drift = advection * speed[1:-1]
    new_heat = (
        heat[1:-1] + heat_diffusion * laplacian(temp) - drift * (heat[1:-1] - heat[:-2])
    )
    new_solute = (
        solute[1:-1]
        + solute_diffusion * laplacian(solute)
        - drift * (solute[1:-1] - solute[:-2])
        + segregation * mushy[1:-1] * (temp[1:-1] - solute[1:-1])
    )
    return new_heat, new_solute


def split(values):
    high = values.astype(jnp.bfloat16)
    low = (values - high.astype(jnp.float32)).astype(jnp.bfloat16)
    return high, low


def split_three(values):
    parts = []
    for _ in range(3):
        part = values.astype(jnp.bfloat16).astype(jnp.float32)
        parts.append(part)
        values = values - part
    return parts


def inverse_factor(matrix_ref):
    order = matrix_ref.shape[0]
    lane = lax.broadcasted_iota(jnp.int32, (PANEL, order), 1)
    sub = lax.broadcasted_iota(jnp.int32, (PANEL, order), 0)
    rows = lax.broadcasted_iota(jnp.int32, (order, order), 0)
    lanes = lax.broadcasted_iota(jnp.int32, (order, order), 1)

    def panel(block, carry):
        base = pl.multiple_of(block * PANEL, PANEL)
        here = matrix_ref[pl.ds(base, PANEL), :]
        cols = [
            jnp.broadcast_to(
                jnp.sum(jnp.where(lane == base + s, here, 0.0), axis=1, keepdims=True),
                (PANEL, order),
            )
            for s in range(PANEL)
        ]
        upper = jnp.where(lane >= base, here, 0.0)
        inverse = jnp.where(lane < base, here, jnp.where(lane == base + sub, 1.0, 0.0))
        diagonal = jnp.zeros((PANEL, order), jnp.float32)
        for s in range(PANEL):
            pivot = cols[s][s : s + 1]
            diagonal = jnp.where(sub == s, pivot, diagonal)
            factor = jnp.where(sub > s, cols[s] / pivot, 0.0)
            upper = upper - factor * upper[s : s + 1]
            inverse = inverse - factor * inverse[s : s + 1]
            for t in range(s + 1, PANEL):
                cols[t] = cols[t] - factor * cols[t][s : s + 1]
        scale = 1.0 / jnp.sqrt(diagonal)
        upper = upper * scale
        inverse = inverse * scale
        right = jnp.where(lane < base + PANEL, inverse, upper)
        upper_parts = split_three(upper)
        right_parts = split_three(right)
        change = lax.dot_general(
            jnp.concatenate([upper_parts[i] for i in (0, 0, 1, 1, 0, 2)], axis=0).astype(jnp.bfloat16),
            jnp.concatenate([right_parts[i] for i in (0, 1, 0, 1, 2, 0)], axis=0).astype(jnp.bfloat16),
            (((0,), (0,)), ((), ())),
            preferred_element_type=jnp.float32,
        )
        old = matrix_ref[...]
        kept = jnp.where((lanes >= base) & (lanes < base + PANEL), 0.0, old)
        matrix_ref[...] = jnp.where(rows >= base + PANEL, kept - change, old)
        matrix_ref[pl.ds(base, PANEL), :] = inverse
        return carry

    lax.fori_loop(0, order // PANEL, panel, 0)


def kernel(
    slabs, halves,
    hc_ref, v_ref, phase_ref, cell_ref, datum_ref, deviate_ref,
    out_hc_ref, out_v_ref,
    mask_ref, index_ref, value_ref, error_ref, hc, vel, raw, mushy, own, other, sums, sums_in, part, seen, square,
    in_sem, halo_send, halo_recv, state_send, state_recv, part_send, part_recv, seen_send, seen_recv, sum_send, sum_recv,
):
    members = own.shape[2]
    width = own.shape[3]
    depth = own.shape[1]
    groups = members // 8
    ens = members * halves
    slab = lax.axis_index("space")
    half = lax.axis_index("mem")
    first = slab == 0
    last = slab == slabs - 1

    load_v = pltpu.make_async_copy(v_ref, vel, in_sem.at[0])
    load_hc = pltpu.make_async_copy(hc_ref, hc, in_sem.at[1])
    load_mask = pltpu.make_async_copy(phase_ref, mask_ref, in_sem.at[2])
    load_observed = [
        pltpu.make_async_copy(cell_ref, index_ref, in_sem.at[3]),
        pltpu.make_async_copy(datum_ref, value_ref, in_sem.at[4]),
        pltpu.make_async_copy(deviate_ref, error_ref, in_sem.at[5]),
    ]
    load_mask.start()
    load_v.start()
    load_hc.start()
    for load in load_observed:
        load.start()

    barrier = pltpu.get_barrier_semaphore()

    def greet(step, carry):
        pl.semaphore_signal(
            barrier, inc=1, device_id=(lax.rem(slab + step, slabs), half), device_id_type=MESH
        )
        return carry

    for hop in range(1, halves):
        pl.semaphore_signal(
            barrier, inc=1, device_id=(slab, lax.rem(half + hop, halves)), device_id_type=MESH
        )
    lax.fori_loop(1, slabs, greet, 0)

    load_mask.wait()
    for z in range(depth):
        row = mask_ref[z : z + 1, :].astype(jnp.float32)
        mushy[z + 2] = jnp.broadcast_to(row, (8, width))

    def relayout_speed(zs):
        for z in zs:
            raw[SPEED, z + 2] = vel[pl.ds(z, members, stride=depth), :]

    def relayout_pair(zs):
        for z in zs:
            raw[HEAT, z + 2] = hc[pl.ds(z, members, stride=2 * depth), :]
            raw[SOLUTE, z + 2] = hc[pl.ds(depth + z, members, stride=2 * depth), :]

    load_v.wait()
    relayout_speed(range(depth))

    def inner_speed(group, carry):
        at = pl.ds(pl.multiple_of(group * 8, 8), 8)
        mask = mushy[2 : depth + 2]
        speed = advance_speed(raw[SPEED, 2 : depth + 2, at, :], mask)
        own[SPEED, 2 : depth - 2, at, :] = advance_speed(speed, mask[1:-1])
        return carry

    lax.fori_loop(0, groups, inner_speed, 0)
    pieces = []

    def send(field, start, count):
        number = len(pieces)
        copies = []
        for hop in range(1, halves):
            copies.append(
                pltpu.make_async_remote_copy(
                    src_ref=own.at[field, pl.ds(start, count)],
                    dst_ref=other.at[hop - 1, field, pl.ds(start, count)],
                    send_sem=state_send.at[hop - 1, number],
                    recv_sem=state_recv.at[hop - 1, number],
                    device_id=(slab, lax.rem(half + hop, halves)),
                    device_id_type=MESH,
                )
            )
        for hop, copy in enumerate(copies, 1):
            pl.when(half + hop < halves)(copy.start)
        pieces.append((field, start, count, copies))

    middle = depth // 2
    pl.semaphore_wait(barrier, slabs + halves - 2)
    send(SPEED, 2, depth - 4)
    load_hc.wait()
    relayout_pair((0, 1, depth - 2, depth - 1))

    def halo(direction, source, target, to, part):
        ref = raw if part == 0 else mushy
        pick = (lambda r, a: r.at[:, pl.ds(a, 2)]) if part == 0 else (lambda r, a: r.at[pl.ds(a, 2)])
        return pltpu.make_async_remote_copy(
            src_ref=pick(ref, source),
            dst_ref=pick(ref, target),
            send_sem=halo_send.at[direction, part],
            recv_sem=halo_recv.at[direction, part],
            device_id=(to, half),
            device_id_type=MESH,
        )

    up = [halo(0, 2, depth + 2, lax.rem(slab + slabs - 1, slabs), part) for part in range(2)]
    down = [halo(1, depth, 0, lax.rem(slab + 1, slabs), part) for part in range(2)]

    @pl.when(first)
    def _():
        raw[:, 0:2] = jnp.zeros((3, 2, members, width), jnp.float32)
        mushy[0:2] = jnp.zeros((2, 8, width), jnp.float32)

    @pl.when(last)
    def _():
        raw[:, depth + 2 : depth + 4] = jnp.zeros((3, 2, members, width), jnp.float32)
        mushy[depth + 2 : depth + 4] = jnp.zeros((2, 8, width), jnp.float32)

    @pl.when(jnp.logical_not(first))
    def _():
        for copy in up:
            copy.start()

    @pl.when(jnp.logical_not(last))
    def _():
        for copy in down:
            copy.start()

    middle = depth // 2
    relayout_pair(range(2, depth - 2))

    def inner_pair(group, carry):
        at = pl.ds(pl.multiple_of(group * 8, 8), 8)
        mask = mushy[2 : depth + 2]
        before = raw[SPEED, 2 : depth + 2, at, :]
        heat, solute = advance_pair(
            raw[HEAT, 2 : depth + 2, at, :], raw[SOLUTE, 2 : depth + 2, at, :], before, mask
        )
        heat, solute = advance_pair(heat, solute, advance_speed(before, mask), mask[1:-1])
        own[HEAT, 2 : depth - 2, at, :] = heat
        own[SOLUTE, 2 : depth - 2, at, :] = solute
        return carry

    lax.fori_loop(0, groups, inner_pair, 0)
    send(HEAT, 2, middle - 2)

    @pl.when(jnp.logical_not(last))
    def _():
        for copy in up:
            copy.wait_recv()

    @pl.when(jnp.logical_not(first))
    def _():
        for copy in down:
            copy.wait_recv()

    def edges(group, carry):
        at = pl.ds(pl.multiple_of(group * 8, 8), 8)
        for begin, outside, edge in ((0, first, 0), (depth - 2, last, 3)):
            mask = mushy[begin : begin + 6]
            before = raw[SPEED, begin : begin + 6, at, :]
            heat, solute = advance_pair(
                raw[HEAT, begin : begin + 6, at, :], raw[SOLUTE, begin : begin + 6, at, :], before, mask
            )
            speed = advance_speed(before, mask)
            row = lax.broadcasted_iota(jnp.int32, heat.shape, 0)
            beyond = jnp.logical_and(row == edge, outside)
            heat, solute, speed = [jnp.where(beyond, 0.0, q) for q in (heat, solute, speed)]
            mask = mask[1:-1]
            new_heat, new_solute = advance_pair(heat, solute, speed, mask)
            own[HEAT, begin : begin + 2, at, :] = new_heat
            own[SOLUTE, begin : begin + 2, at, :] = new_solute
            own[SPEED, begin : begin + 2, at, :] = advance_speed(speed, mask)
        return carry

    lax.fori_loop(0, groups, edges, 0)

    lane = lax.broadcasted_iota(jnp.int32, (members, width), 1)
    per_slab = index_ref.shape[0]
    for load in load_observed:
        load.wait()
    observed = jnp.zeros((members, width), jnp.float32)
    value = jnp.zeros((members, width), jnp.float32)
    error = jnp.ones((members, width), jnp.float32)
    for o in range(per_slab):
        cell = index_ref[o]
        z = cell // width
        w = cell - z * width
        factor = 1.0 - mushy[z + 2][0:1] * (1.0 - mushy_ratio)
        temp = jnp.where(lane == w, own[HEAT, z] * factor, 0.0)
        observed = jnp.where(lane == o, jnp.sum(temp, axis=1, keepdims=True), observed)
        value = jnp.where(lane == o, value_ref[o], value)
        error = jnp.where(lane == o, error_ref[o], error)
    square[...] = jnp.zeros((ens, width), jnp.float32)
    square[pl.ds(pl.multiple_of(half * members, 8), members), :] = (observed - value) / error
    turned = square[...].T
    part[half] = turned[0:8] + pltpu.roll(turned[8:16], ens // 2, 1)
    part_copies = [
        pltpu.make_async_remote_copy(
            src_ref=part.at[half],
            dst_ref=part.at[half],
            send_sem=part_send.at[hop - 1],
            recv_sem=part_recv.at[0],
            device_id=(slab, lax.rem(half + hop, halves)),
            device_id_type=MESH,
        )
        for hop in range(1, halves)
    ]
    for copy in part_copies:
        copy.start()

    send(SPEED, 0, 2)
    send(SPEED, depth - 2, 2)
    send(HEAT, 0, 2)
    send(HEAT, middle, middle)
    send(SOLUTE, 0, middle)
    send(SOLUTE, middle, middle - 4)
    send(SOLUTE, depth - 4, 2)
    send(SOLUTE, depth - 2, 2)

    others = part.at[pl.ds(0, halves - 1)]
    pltpu.make_async_copy(others, others, part_recv.at[0]).wait()
    place = lax.broadcasted_iota(jnp.int32, (8, ens), 1)
    low = jnp.zeros((8, ens), jnp.float32)
    high = jnp.zeros((8, ens), jnp.float32)
    for m in range(halves):
        mine = (place >= m * members) & (place < (m + 1) * members)
        low = jnp.where(mine, part[m], low)
        high = jnp.where(mine, pltpu.roll(part[m], ens // 2, 1), high)
    seen[slab, 0:8] = low
    seen[slab, 8:16] = high

    def tell(step, carry):
        pltpu.make_async_remote_copy(
            src_ref=seen.at[slab],
            dst_ref=seen.at[slab],
            send_sem=seen_send.at[0],
            recv_sem=seen_recv.at[0],
            device_id=(lax.rem(slab + step, slabs), half),
            device_id_type=MESH,
        ).start()
        return carry

    lax.fori_loop(1, slabs, tell, 0)

    for hop in range(1, halves):

        @pl.when(half < hop)
        def _():
            other[hop - 1, :, :, 8:, :] = jnp.zeros((3, depth, members - 8, width), jnp.float32)

    rest = seen.at[pl.ds(0, slabs - 1)]
    pltpu.make_async_copy(rest, rest, seen_recv.at[0]).wait()

    deviation = seen[...].reshape(slabs * 16, ens)
    mean = jnp.sum(deviation, axis=1, keepdims=True) * (1.0 / ens)
    root = 1.0 / (ens - 1.0) ** 0.5
    spread = (deviation - mean) * root
    project = -jnp.sum(spread * mean, axis=0, keepdims=True)
    gram = lax.dot_general(
        spread, spread, (((0,), (0,)), ((), ())),
        precision=HIGHEST, preferred_element_type=jnp.float32,
    )
    rows = lax.broadcasted_iota(jnp.int32, (ens, ens), 0)
    lanes = lax.broadcasted_iota(jnp.int32, (ens, ens), 1)
    square[...] = jnp.where(rows == lanes, 1.0, 0.0) + gram
    inverse_factor(square)
    inverse = square[...]
    shift = jnp.sum(inverse * project, axis=1, keepdims=True)
    shift = jnp.sum(inverse * shift, axis=0, keepdims=True)
    combined = inverse + shift * root
    level = (1.0 - jnp.sum(combined, axis=1, keepdims=True)) * (1.0 / ens)
    combined = combined + level
    shift_column = jnp.sum(jnp.where(rows == lanes, shift, 0.0), axis=1, keepdims=True) * root
    square[...] = jnp.broadcast_to(shift_column, (ens, width))
    own_rows = pl.ds(pl.multiple_of(half * members, 8), members)

    @pl.when(half > 0)
    def _():
        own_shift = square[own_rows, :]
        for z in range(depth):
            for field in range(3):
                state = own[field, z]
                sums[field, 0, z : z + 1, :] = jnp.sum(state, axis=0, keepdims=True)
                sums[field, 1, z : z + 1, :] = jnp.sum(state * own_shift, axis=0, keepdims=True)

    sum_copies = [
        pltpu.make_async_remote_copy(
            src_ref=sums,
            dst_ref=sums_in.at[hop - 1],
            send_sem=sum_send.at[hop - 1],
            recv_sem=sum_recv.at[hop - 1],
            device_id=(slab, lax.rem(half + hop, halves)),
            device_id_type=MESH,
        )
        for hop in range(1, halves)
    ]
    for hop, copy in enumerate(sum_copies, 1):
        pl.when(half + hop >= halves)(copy.start)

    combined = pltpu.roll(combined, lax.rem(ens - half * members, ens), 1)
    ahead = lanes // members
    at = lanes - ahead * members
    of_sums = jnp.where(at == 0, level, jnp.where(at == 1, 1.0, 0.0))
    square[...] = jnp.where((ahead > 0) & (half + ahead < halves), of_sums, combined)
    weights = square[own_rows, :]

    def stack(part):
        part_high, part_low = split(part)
        return jnp.concatenate([part_high, part_high, part_low], axis=1)

    own_weights = stack(weights[:, :members])
    other_weights = stack(weights[:, members:])

    def mix(field, z, blocks, chosen, add):
        parts = [jnp.concatenate(blocks(d), axis=0) for d in (z, z + 1)]
        state_high, state_low = split(jnp.concatenate(parts, axis=1))
        mixed = jnp.dot(
            chosen,
            jnp.concatenate([state_high, state_low, state_high], axis=0),
            preferred_element_type=jnp.float32,
        )
        for i, d in enumerate((z, z + 1)):
            block = mixed[:, i * width : (i + 1) * width]
            if field == SPEED:
                out, at = out_v_ref, pl.ds(d, members, stride=depth)
            else:
                out, at = out_hc_ref, pl.ds(field * depth + d, members, stride=2 * depth)
            out[at, :] = out[at, :] + block if add else block

    for field in range(3):
        for z in range(0, depth, 2):
            mix(field, z, lambda d: [own[field, d]], own_weights, False)

    for hop, copy in enumerate(sum_copies, 1):

        @pl.when(half < hop)
        def _():
            copy.wait_recv()
            sub = lax.broadcasted_iota(jnp.int32, (8, width), 0)
            for field in range(3):
                for z in range(depth):
                    plain = sums_in[hop - 1, field, 0, z : z + 1, :]
                    shifted = sums_in[hop - 1, field, 1, z : z + 1, :]
                    other[hop - 1, field, z, 0:8, :] = jnp.where(
                        sub == 0, plain, jnp.where(sub == 1, shifted, 0.0)
                    )

    for field, start, count, copies in pieces:
        for hop, copy in enumerate(copies, 1):
            pl.when(half >= hop)(copy.wait_recv)
        for z in range(start, start + count, 2):
            mix(
                field,
                z,
                lambda d: [other[halves - q - 1, field, d] for q in range(1, halves)],
                other_weights,
                True,
            )

    for _, _, _, copies in pieces:
        for hop, copy in enumerate(copies, 1):
            pl.when(half + hop < halves)(copy.wait_send)
    for hop, copy in enumerate(sum_copies, 1):
        pl.when(half + hop >= halves)(copy.wait_send)
    for copy in part_copies:
        copy.wait_send()
    pltpu.make_async_copy(rest, rest, seen_send.at[0]).wait()

    @pl.when(jnp.logical_not(first))
    def _():
        for copy in up:
            copy.wait_send()

    @pl.when(jnp.logical_not(last))
    def _():
        for copy in down:
            copy.wait_send()


def write_back(hc, vel, out_hc, out_vel, sem):
    copies = []
    for source, target, count in ((hc, out_hc, 4), (vel, out_vel, 2)):
        rows = source.shape[0] // count
        for i in range(count):
            at = pl.ds(i * rows, rows)
            copies.append(
                pltpu.make_async_copy(source.at[at], target.at[at], sem.at[len(copies)])
            )
    for copy in copies:
        copy.start()
    for copy in copies:
        copy.wait()


def on_device(slabs, halves, member_heat_solute, velocity, phase_mask, obs_index, obs_value, obs_error):
    members, _, depth, width = member_heat_solute.shape
    ens = members * halves
    held = pl.BlockSpec(memory_space=pltpu.VMEM)
    anywhere = pl.BlockSpec(memory_space=pltpu.HBM)
    hc, vel = pl.pallas_call(
        functools.partial(kernel, slabs, halves),
        out_shape=(
            pltpu.VMEM((members * 2 * depth, width), jnp.float32),
            pltpu.VMEM((members * depth, width), jnp.float32),
        ),
        in_specs=[anywhere] * 6,
        out_specs=(held, held),
        scratch_shapes=[
            pltpu.VMEM((depth, width), jnp.int32),
            pltpu.SMEM(obs_index.shape, jnp.int32),
            pltpu.SMEM(obs_value.shape, jnp.float32),
            pltpu.SMEM(obs_error.shape, jnp.float32),
            pltpu.VMEM((members * 2 * depth, width), jnp.float32),
            pltpu.VMEM((members * depth, width), jnp.float32),
            pltpu.VMEM((3, depth + 4, members, width), jnp.float32),
            pltpu.VMEM((depth + 4, 8, width), jnp.float32),
            pltpu.VMEM((3, depth, members, width), jnp.float32),
            pltpu.VMEM((halves - 1, 3, depth, members, width), jnp.float32),
            pltpu.VMEM((3, 2, depth, width), jnp.float32),
            pltpu.VMEM((halves - 1, 3, 2, depth, width), jnp.float32),
            pltpu.VMEM((halves, 8, ens), jnp.float32),
            pltpu.VMEM((slabs, 16, ens), jnp.float32),
            pltpu.VMEM((ens, ens), jnp.float32),
            pltpu.SemaphoreType.DMA((6,)),
            pltpu.SemaphoreType.DMA((2, 2)),
            pltpu.SemaphoreType.DMA((2, 2)),
            pltpu.SemaphoreType.DMA((halves - 1, 10)),
            pltpu.SemaphoreType.DMA((halves - 1, 10)),
            pltpu.SemaphoreType.DMA((halves - 1,)),
            pltpu.SemaphoreType.DMA((1,)),
            pltpu.SemaphoreType.DMA((1,)),
            pltpu.SemaphoreType.DMA((1,)),
            pltpu.SemaphoreType.DMA((halves - 1,)),
            pltpu.SemaphoreType.DMA((halves - 1,)),
        ],
        compiler_params=pltpu.CompilerParams(
            collective_id=0, has_side_effects=True, vmem_limit_bytes=40 * 1024 * 1024
        ),
    )(
        *[
            pltpu.with_memory_space_constraint(x, pltpu.HBM)
            for x in (
                member_heat_solute.reshape(-1, width),
                velocity.reshape(-1, width),
                phase_mask,
                obs_index,
                obs_value,
                obs_error,
            )
        ]
    )
    hc, vel = pl.pallas_call(
        write_back,
        out_shape=(
            jax.ShapeDtypeStruct(hc.shape, jnp.float32),
            jax.ShapeDtypeStruct(vel.shape, jnp.float32),
        ),
        in_specs=[held, held],
        out_specs=(anywhere, anywhere),
        scratch_shapes=[pltpu.SemaphoreType.DMA((6,))],
        compiler_params=pltpu.CompilerParams(vmem_limit_bytes=16 * 1024 * 1024),
    )(
        pltpu.with_memory_space_constraint(hc, pltpu.VMEM),
        pltpu.with_memory_space_constraint(vel, pltpu.VMEM),
    )
    return hc.reshape(members, 2, depth, width), vel.reshape(members, depth, width)


def solution(mesh):
    return jax.shard_map(
        functools.partial(on_device, mesh.shape["space"], mesh.shape["mem"]),
        mesh=mesh,
        in_specs=(
            P("mem", None, "space", None),
            P("mem", "space", None),
            P("space", None),
            P("space"),
            P("space"),
            P("space"),
        ),
        out_specs=(P("mem", None, "space", None), P("mem", "space", None)),
        check_vma=False,
    )
```

```python
import functools

import jax
import jax.numpy as jnp
from jax import lax
from jax.experimental import pallas as pl
from jax.experimental.pallas import tpu as pltpu
from jax.sharding import PartitionSpec as P

heat_diffusion = 0.15
advection = 0.4
solute_diffusion = 0.05
segregation = 0.3
momentum_diffusion = 0.1
darcy_drag = 0.5
mushy_ratio = 1.0 / 3.0

MESH = pl.DeviceIdType.MESH
HIGHEST = lax.Precision.HIGHEST
HEAT, SOLUTE, SPEED = 0, 1, 2
PANEL = 16


def lateral_sum(field):
    lane = lax.broadcasted_iota(jnp.int32, field.shape, 2)
    last = field.shape[2] - 1
    left = jnp.where(lane == 0, field, pltpu.roll(field, 1, 2))
    right = jnp.where(lane == last, field, pltpu.roll(field, last, 2))
    return left + right


def laplacian(field):
    centre = field[1:-1]
    return field[2:] + field[:-2] + lateral_sum(centre) - 4.0 * centre


def advance_speed(speed, mushy):
    centre = speed[1:-1]
    return centre + momentum_diffusion * laplacian(speed) - darcy_drag * mushy[1:-1] * centre


def advance_pair(heat, solute, speed, mushy):
    temp = heat * (1.0 - mushy * (1.0 - mushy_ratio))
    drift = advection * speed[1:-1]
    new_heat = (
        heat[1:-1] + heat_diffusion * laplacian(temp) - drift * (heat[1:-1] - heat[:-2])
    )
    new_solute = (
        solute[1:-1]
        + solute_diffusion * laplacian(solute)
        - drift * (solute[1:-1] - solute[:-2])
        + segregation * mushy[1:-1] * (temp[1:-1] - solute[1:-1])
    )
    return new_heat, new_solute


def split(values):
    high = values.astype(jnp.bfloat16)
    low = (values - high.astype(jnp.float32)).astype(jnp.bfloat16)
    return high, low


def split_three(values):
    parts = []
    for _ in range(3):
        part = values.astype(jnp.bfloat16).astype(jnp.float32)
        parts.append(part)
        values = values - part
    return parts


def inverse_factor(matrix_ref):
    order = matrix_ref.shape[0]
    lane = lax.broadcasted_iota(jnp.int32, (PANEL, order), 1)
    sub = lax.broadcasted_iota(jnp.int32, (PANEL, order), 0)
    rows = lax.broadcasted_iota(jnp.int32, (order, order), 0)
    lanes = lax.broadcasted_iota(jnp.int32, (order, order), 1)

    def panel(block, carry):
        base = pl.multiple_of(block * PANEL, PANEL)
        here = matrix_ref[pl.ds(base, PANEL), :]
        cols = [
            jnp.broadcast_to(
                jnp.sum(jnp.where(lane == base + s, here, 0.0), axis=1, keepdims=True),
                (PANEL, order),
            )
            for s in range(PANEL)
        ]
        upper = jnp.where(lane >= base, here, 0.0)
        inverse = jnp.where(lane < base, here, jnp.where(lane == base + sub, 1.0, 0.0))
        diagonal = jnp.zeros((PANEL, order), jnp.float32)
        for s in range(PANEL):
            pivot = cols[s][s : s + 1]
            diagonal = jnp.where(sub == s, pivot, diagonal)
            factor = jnp.where(sub > s, cols[s] / pivot, 0.0)
            upper = upper - factor * upper[s : s + 1]
            inverse = inverse - factor * inverse[s : s + 1]
            for t in range(s + 1, PANEL):
                cols[t] = cols[t] - factor * cols[t][s : s + 1]
        scale = 1.0 / jnp.sqrt(diagonal)
        upper = upper * scale
        inverse = inverse * scale
        right = jnp.where(lane < base + PANEL, inverse, upper)
        upper_parts = split_three(upper)
        right_parts = split_three(right)
        change = lax.dot_general(
            jnp.concatenate([upper_parts[i] for i in (0, 0, 1, 1, 0, 2)], axis=0).astype(jnp.bfloat16),
            jnp.concatenate([right_parts[i] for i in (0, 1, 0, 1, 2, 0)], axis=0).astype(jnp.bfloat16),
            (((0,), (0,)), ((), ())),
            preferred_element_type=jnp.float32,
        )
        old = matrix_ref[...]
        kept = jnp.where((lanes >= base) & (lanes < base + PANEL), 0.0, old)
        matrix_ref[...] = jnp.where(rows >= base + PANEL, kept - change, old)
        matrix_ref[pl.ds(base, PANEL), :] = inverse
        return carry

    lax.fori_loop(0, order // PANEL, panel, 0)


def kernel(
    slabs, halves,
    hc_ref, v_ref, phase_ref, cell_ref, datum_ref, deviate_ref,
    out_hc_ref, out_v_ref,
    mask_ref, index_ref, value_ref, error_ref, hc, vel, raw, mushy, own, other, sums, sums_in, part, seen, square,
    in_sem, halo_send, halo_recv, state_send, state_recv, part_send, part_recv, seen_send, seen_recv, sum_send, sum_recv,
):
    members = own.shape[2]
    width = own.shape[3]
    depth = own.shape[1]
    groups = members // 8
    ens = members * halves
    slab = lax.axis_index("space")
    half = lax.axis_index("mem")
    first = slab == 0
    last = slab == slabs - 1

    load_v = pltpu.make_async_copy(v_ref, vel, in_sem.at[0])
    load_hc = pltpu.make_async_copy(hc_ref, hc, in_sem.at[1])
    load_mask = pltpu.make_async_copy(phase_ref, mask_ref, in_sem.at[2])
    load_observed = [
        pltpu.make_async_copy(cell_ref, index_ref, in_sem.at[3]),
        pltpu.make_async_copy(datum_ref, value_ref, in_sem.at[4]),
        pltpu.make_async_copy(deviate_ref, error_ref, in_sem.at[5]),
    ]
    load_v.start()
    load_mask.start()

    barrier = pltpu.get_barrier_semaphore()

    def greet(step, carry):
        pl.semaphore_signal(
            barrier, inc=1, device_id=(lax.rem(slab + step, slabs), half), device_id_type=MESH
        )
        return carry

    for hop in range(1, halves):
        pl.semaphore_signal(
            barrier, inc=1, device_id=(slab, lax.rem(half + hop, halves)), device_id_type=MESH
        )
    lax.fori_loop(1, slabs, greet, 0)
    load_hc.start()
    for load in load_observed:
        load.start()

    load_mask.wait()
    for z in range(depth):
        row = mask_ref[z : z + 1, :].astype(jnp.float32)
        mushy[z + 2] = jnp.broadcast_to(row, (8, width))

    def relayout_speed(start, count):
        for z in range(depth):
            raw[SPEED, z + 2, start : start + count, :] = vel[
                pl.ds(start * depth + z, count, stride=depth), :
            ]

    def relayout_pair(zs):
        for z in zs:
            raw[HEAT, z + 2] = hc[pl.ds(z, members, stride=2 * depth), :]
            raw[SOLUTE, z + 2] = hc[pl.ds(depth + z, members, stride=2 * depth), :]

    load_v.wait()

    def inner_speed(group, carry):
        at = pl.ds(pl.multiple_of(group * 8, 8), 8)
        mask = mushy[2 : depth + 2]
        speed = advance_speed(raw[SPEED, 2 : depth + 2, at, :], mask)
        own[SPEED, 2 : depth - 2, at, :] = advance_speed(speed, mask[1:-1])
        return carry

    pieces = []

    def send(field, start, count, first_member=0, some=members, mixed=True):
        number = len(pieces)
        copies = []
        for hop in range(1, halves):
            copies.append(
                pltpu.make_async_remote_copy(
                    src_ref=own.at[field, pl.ds(start, count), pl.ds(first_member, some)],
                    dst_ref=other.at[
                        hop - 1, field, pl.ds(start, count), pl.ds(first_member, some)
                    ],
                    send_sem=state_send.at[hop - 1, number],
                    recv_sem=state_recv.at[hop - 1, number],
                    device_id=(slab, lax.rem(half + hop, halves)),
                    device_id_type=MESH,
                )
            )
        for hop, copy in enumerate(copies, 1):
            pl.when(half + hop < halves)(copy.start)
        pieces.append((field, start, count if mixed else 0, copies))

    middle = depth // 2
    some = members // 2
    relayout_speed(0, some)
    lax.fori_loop(0, groups // 2, inner_speed, 0)
    pl.semaphore_wait(barrier, slabs + halves - 2)
    send(SPEED, 2, depth - 4, 0, some, mixed=False)
    relayout_speed(some, some)
    lax.fori_loop(groups // 2, groups, inner_speed, 0)
    send(SPEED, 2, depth - 4, some, some)
    load_hc.wait()
    relayout_pair((0, 1, depth - 2, depth - 1))

    def halo(direction, source, target, to, part):
        ref = raw if part == 0 else mushy
        pick = (lambda r, a: r.at[:, pl.ds(a, 2)]) if part == 0 else (lambda r, a: r.at[pl.ds(a, 2)])
        return pltpu.make_async_remote_copy(
            src_ref=pick(ref, source),
            dst_ref=pick(ref, target),
            send_sem=halo_send.at[direction, part],
            recv_sem=halo_recv.at[direction, part],
            device_id=(to, half),
            device_id_type=MESH,
        )

    up = [halo(0, 2, depth + 2, lax.rem(slab + slabs - 1, slabs), part) for part in range(2)]
    down = [halo(1, depth, 0, lax.rem(slab + 1, slabs), part) for part in range(2)]

    @pl.when(first)
    def _():
        raw[:, 0:2] = jnp.zeros((3, 2, members, width), jnp.float32)
        mushy[0:2] = jnp.zeros((2, 8, width), jnp.float32)

    @pl.when(last)
    def _():
        raw[:, depth + 2 : depth + 4] = jnp.zeros((3, 2, members, width), jnp.float32)
        mushy[depth + 2 : depth + 4] = jnp.zeros((2, 8, width), jnp.float32)

    @pl.when(jnp.logical_not(first))
    def _():
        for copy in up:
            copy.start()

    @pl.when(jnp.logical_not(last))
    def _():
        for copy in down:
            copy.start()

    relayout_pair(range(2, depth - 2))

    def inner_pair(group, carry):
        at = pl.ds(pl.multiple_of(group * 8, 8), 8)
        mask = mushy[2 : depth + 2]
        before = raw[SPEED, 2 : depth + 2, at, :]
        heat, solute = advance_pair(
            raw[HEAT, 2 : depth + 2, at, :], raw[SOLUTE, 2 : depth + 2, at, :], before, mask
        )
        heat, solute = advance_pair(heat, solute, advance_speed(before, mask), mask[1:-1])
        own[HEAT, 2 : depth - 2, at, :] = heat
        own[SOLUTE, 2 : depth - 2, at, :] = solute
        return carry

    lax.fori_loop(0, groups, inner_pair, 0)
    send(HEAT, 2, middle - 2)

    @pl.when(jnp.logical_not(last))
    def _():
        for copy in up:
            copy.wait_recv()

    @pl.when(jnp.logical_not(first))
    def _():
        for copy in down:
            copy.wait_recv()

    def edges(group, carry):
        at = pl.ds(pl.multiple_of(group * 8, 8), 8)
        for begin, outside, edge in ((0, first, 0), (depth - 2, last, 3)):
            mask = mushy[begin : begin + 6]
            before = raw[SPEED, begin : begin + 6, at, :]
            heat, solute = advance_pair(
                raw[HEAT, begin : begin + 6, at, :], raw[SOLUTE, begin : begin + 6, at, :], before, mask
            )
            speed = advance_speed(before, mask)
            row = lax.broadcasted_iota(jnp.int32, heat.shape, 0)
            beyond = jnp.logical_and(row == edge, outside)
            heat, solute, speed = [jnp.where(beyond, 0.0, q) for q in (heat, solute, speed)]
            mask = mask[1:-1]
            new_heat, new_solute = advance_pair(heat, solute, speed, mask)
            own[HEAT, begin : begin + 2, at, :] = new_heat
            own[SOLUTE, begin : begin + 2, at, :] = new_solute
            own[SPEED, begin : begin + 2, at, :] = advance_speed(speed, mask)
        return carry

    lax.fori_loop(0, groups, edges, 0)

    lane = lax.broadcasted_iota(jnp.int32, (members, width), 1)
    per_slab = index_ref.shape[0]
    for load in load_observed:
        load.wait()
    observed = jnp.zeros((members, width), jnp.float32)
    value = jnp.zeros((members, width), jnp.float32)
    error = jnp.ones((members, width), jnp.float32)
    for o in range(per_slab):
        cell = index_ref[o]
        z = cell // width
        w = cell - z * width
        factor = 1.0 - mushy[z + 2][0:1] * (1.0 - mushy_ratio)
        temp = jnp.where(lane == w, own[HEAT, z] * factor, 0.0)
        observed = jnp.where(lane == o, jnp.sum(temp, axis=1, keepdims=True), observed)
        value = jnp.where(lane == o, value_ref[o], value)
        error = jnp.where(lane == o, error_ref[o], error)
    square[...] = jnp.zeros((ens, width), jnp.float32)
    square[pl.ds(pl.multiple_of(half * members, 8), members), :] = (observed - value) / error
    turned = square[...].T
    part[half] = turned[0:8] + pltpu.roll(turned[8:16], ens // 2, 1)
    part_copies = [
        pltpu.make_async_remote_copy(
            src_ref=part.at[half],
            dst_ref=part.at[half],
            send_sem=part_send.at[hop - 1],
            recv_sem=part_recv.at[0],
            device_id=(slab, lax.rem(half + hop, halves)),
            device_id_type=MESH,
        )
        for hop in range(1, halves)
    ]
    for copy in part_copies:
        copy.start()

    send(SPEED, 0, 2)
    send(SPEED, depth - 2, 2)
    send(HEAT, 0, 2)
    send(HEAT, middle, middle)
    send(SOLUTE, 0, middle)
    send(SOLUTE, middle, middle - 4)
    send(SOLUTE, depth - 4, 2)
    send(SOLUTE, depth - 2, 2)

    others = part.at[pl.ds(0, halves - 1)]
    pltpu.make_async_copy(others, others, part_recv.at[0]).wait()
    place = lax.broadcasted_iota(jnp.int32, (8, ens), 1)
    low = jnp.zeros((8, ens), jnp.float32)
    high = jnp.zeros((8, ens), jnp.float32)
    for m in range(halves):
        mine = (place >= m * members) & (place < (m + 1) * members)
        low = jnp.where(mine, part[m], low)
        high = jnp.where(mine, pltpu.roll(part[m], ens // 2, 1), high)
    seen[slab, 0:8] = low
    seen[slab, 8:16] = high

    def tell(step, carry):
        pltpu.make_async_remote_copy(
            src_ref=seen.at[slab],
            dst_ref=seen.at[slab],
            send_sem=seen_send.at[0],
            recv_sem=seen_recv.at[0],
            device_id=(lax.rem(slab + step, slabs), half),
            device_id_type=MESH,
        ).start()
        return carry

    lax.fori_loop(1, slabs, tell, 0)

    for hop in range(1, halves):

        @pl.when(half < hop)
        def _():
            other[hop - 1, :, :, 8:, :] = jnp.zeros((3, depth, members - 8, width), jnp.float32)

    rest = seen.at[pl.ds(0, slabs - 1)]
    pltpu.make_async_copy(rest, rest, seen_recv.at[0]).wait()

    deviation = seen[...].reshape(slabs * 16, ens)
    mean = jnp.sum(deviation, axis=1, keepdims=True) * (1.0 / ens)
    root = 1.0 / (ens - 1.0) ** 0.5
    spread = (deviation - mean) * root
    project = -jnp.sum(spread * mean, axis=0, keepdims=True)
    gram = lax.dot_general(
        spread, spread, (((0,), (0,)), ((), ())),
        precision=HIGHEST, preferred_element_type=jnp.float32,
    )
    rows = lax.broadcasted_iota(jnp.int32, (ens, ens), 0)
    lanes = lax.broadcasted_iota(jnp.int32, (ens, ens), 1)
    square[...] = jnp.where(rows == lanes, 1.0, 0.0) + gram
    inverse_factor(square)
    inverse = square[...]
    shift = jnp.sum(inverse * project, axis=1, keepdims=True)
    shift = jnp.sum(inverse * shift, axis=0, keepdims=True)
    combined = inverse + shift * root
    level = (1.0 - jnp.sum(combined, axis=1, keepdims=True)) * (1.0 / ens)
    combined = combined + level
    shift_column = jnp.sum(jnp.where(rows == lanes, shift, 0.0), axis=1, keepdims=True) * root
    square[...] = jnp.broadcast_to(shift_column, (ens, width))
    own_rows = pl.ds(pl.multiple_of(half * members, 8), members)

    @pl.when(half > 0)
    def _():
        own_shift = square[own_rows, :]
        for z in range(depth):
            for field in range(3):
                state = own[field, z]
                sums[field, 0, z : z + 1, :] = jnp.sum(state, axis=0, keepdims=True)
                sums[field, 1, z : z + 1, :] = jnp.sum(state * own_shift, axis=0, keepdims=True)

    sum_copies = [
        pltpu.make_async_remote_copy(
            src_ref=sums,
            dst_ref=sums_in.at[hop - 1],
            send_sem=sum_send.at[hop - 1],
            recv_sem=sum_recv.at[hop - 1],
            device_id=(slab, lax.rem(half + hop, halves)),
            device_id_type=MESH,
        )
        for hop in range(1, halves)
    ]
    for hop, copy in enumerate(sum_copies, 1):
        pl.when(half + hop >= halves)(copy.start)

    combined = pltpu.roll(combined, lax.rem(ens - half * members, ens), 1)
    ahead = lanes // members
    at = lanes - ahead * members
    of_sums = jnp.where(at == 0, level, jnp.where(at == 1, 1.0, 0.0))
    square[...] = jnp.where((ahead > 0) & (half + ahead < halves), of_sums, combined)
    weights = square[own_rows, :]

    def stack(part):
        part_high, part_low = split(part)
        return jnp.concatenate([part_high, part_high, part_low], axis=1)

    own_weights = stack(weights[:, :members])
    other_weights = stack(weights[:, members:])

    def mix(field, z, blocks, chosen, add):
        parts = [jnp.concatenate(blocks(d), axis=0) for d in (z, z + 1)]
        state_high, state_low = split(jnp.concatenate(parts, axis=1))
        mixed = jnp.dot(
            chosen,
            jnp.concatenate([state_high, state_low, state_high], axis=0),
            preferred_element_type=jnp.float32,
        )
        for i, d in enumerate((z, z + 1)):
            block = mixed[:, i * width : (i + 1) * width]
            if field == SPEED:
                out, at = out_v_ref, pl.ds(d, members, stride=depth)
            else:
                out, at = out_hc_ref, pl.ds(field * depth + d, members, stride=2 * depth)
            out[at, :] = out[at, :] + block if add else block

    for field in range(3):
        for z in range(0, depth, 2):
            mix(field, z, lambda d: [own[field, d]], own_weights, False)

    for hop, copy in enumerate(sum_copies, 1):

        @pl.when(half < hop)
        def _():
            copy.wait_recv()
            sub = lax.broadcasted_iota(jnp.int32, (8, width), 0)
            for field in range(3):
                for z in range(depth):
                    plain = sums_in[hop - 1, field, 0, z : z + 1, :]
                    shifted = sums_in[hop - 1, field, 1, z : z + 1, :]
                    other[hop - 1, field, z, 0:8, :] = jnp.where(
                        sub == 0, plain, jnp.where(sub == 1, shifted, 0.0)
                    )

    for field, start, count, copies in pieces:
        for hop, copy in enumerate(copies, 1):
            pl.when(half >= hop)(copy.wait_recv)
        for z in range(start, start + count, 2):
            mix(
                field,
                z,
                lambda d: [other[halves - q - 1, field, d] for q in range(1, halves)],
                other_weights,
                True,
            )

    for _, _, _, copies in pieces:
        for hop, copy in enumerate(copies, 1):
            pl.when(half + hop < halves)(copy.wait_send)
    for hop, copy in enumerate(sum_copies, 1):
        pl.when(half + hop >= halves)(copy.wait_send)
    for copy in part_copies:
        copy.wait_send()
    pltpu.make_async_copy(rest, rest, seen_send.at[0]).wait()

    @pl.when(jnp.logical_not(first))
    def _():
        for copy in up:
            copy.wait_send()

    @pl.when(jnp.logical_not(last))
    def _():
        for copy in down:
            copy.wait_send()


def write_back(hc, vel, out_hc, out_vel, sem):
    copies = []
    for source, target, count in ((hc, out_hc, 4), (vel, out_vel, 2)):
        rows = source.shape[0] // count
        for i in range(count):
            at = pl.ds(i * rows, rows)
            copies.append(
                pltpu.make_async_copy(source.at[at], target.at[at], sem.at[len(copies)])
            )
    for copy in copies:
        copy.start()
    for copy in copies:
        copy.wait()


def on_device(slabs, halves, member_heat_solute, velocity, phase_mask, obs_index, obs_value, obs_error):
    members, _, depth, width = member_heat_solute.shape
    ens = members * halves
    held = pl.BlockSpec(memory_space=pltpu.VMEM)
    anywhere = pl.BlockSpec(memory_space=pltpu.HBM)
    hc, vel = pl.pallas_call(
        functools.partial(kernel, slabs, halves),
        out_shape=(
            pltpu.VMEM((members * 2 * depth, width), jnp.float32),
            pltpu.VMEM((members * depth, width), jnp.float32),
        ),
        in_specs=[anywhere] * 6,
        out_specs=(held, held),
        scratch_shapes=[
            pltpu.VMEM((depth, width), jnp.int32),
            pltpu.SMEM(obs_index.shape, jnp.int32),
            pltpu.SMEM(obs_value.shape, jnp.float32),
            pltpu.SMEM(obs_error.shape, jnp.float32),
            pltpu.VMEM((members * 2 * depth, width), jnp.float32),
            pltpu.VMEM((members * depth, width), jnp.float32),
            pltpu.VMEM((3, depth + 4, members, width), jnp.float32),
            pltpu.VMEM((depth + 4, 8, width), jnp.float32),
            pltpu.VMEM((3, depth, members, width), jnp.float32),
            pltpu.VMEM((halves - 1, 3, depth, members, width), jnp.float32),
            pltpu.VMEM((3, 2, depth, width), jnp.float32),
            pltpu.VMEM((halves - 1, 3, 2, depth, width), jnp.float32),
            pltpu.VMEM((halves, 8, ens), jnp.float32),
            pltpu.VMEM((slabs, 16, ens), jnp.float32),
            pltpu.VMEM((ens, ens), jnp.float32),
            pltpu.SemaphoreType.DMA((6,)),
            pltpu.SemaphoreType.DMA((2, 2)),
            pltpu.SemaphoreType.DMA((2, 2)),
            pltpu.SemaphoreType.DMA((halves - 1, 11)),
            pltpu.SemaphoreType.DMA((halves - 1, 11)),
            pltpu.SemaphoreType.DMA((halves - 1,)),
            pltpu.SemaphoreType.DMA((1,)),
            pltpu.SemaphoreType.DMA((1,)),
            pltpu.SemaphoreType.DMA((1,)),
            pltpu.SemaphoreType.DMA((halves - 1,)),
            pltpu.SemaphoreType.DMA((halves - 1,)),
        ],
        compiler_params=pltpu.CompilerParams(
            collective_id=0, has_side_effects=True, vmem_limit_bytes=40 * 1024 * 1024
        ),
    )(
        *[
            pltpu.with_memory_space_constraint(x, pltpu.HBM)
            for x in (
                member_heat_solute.reshape(-1, width),
                velocity.reshape(-1, width),
                phase_mask,
                obs_index,
                obs_value,
                obs_error,
            )
        ]
    )
    hc, vel = pl.pallas_call(
        write_back,
        out_shape=(
            jax.ShapeDtypeStruct(hc.shape, jnp.float32),
            jax.ShapeDtypeStruct(vel.shape, jnp.float32),
        ),
        in_specs=[held, held],
        out_specs=(anywhere, anywhere),
        scratch_shapes=[pltpu.SemaphoreType.DMA((6,))],
        compiler_params=pltpu.CompilerParams(vmem_limit_bytes=16 * 1024 * 1024),
    )(
        pltpu.with_memory_space_constraint(hc, pltpu.VMEM),
        pltpu.with_memory_space_constraint(vel, pltpu.VMEM),
    )
    return hc.reshape(members, 2, depth, width), vel.reshape(members, depth, width)


def solution(mesh):
    return jax.shard_map(
        functools.partial(on_device, mesh.shape["space"], mesh.shape["mem"]),
        mesh=mesh,
        in_specs=(
            P("mem", None, "space", None),
            P("mem", "space", None),
            P("space", None),
            P("space"),
            P("space"),
            P("space"),
        ),
        out_specs=(P("mem", None, "space", None), P("mem", "space", None)),
        check_vma=False,
    )
```
